32 devices in a mesh: dp: 8 (over z, x), tensor: 4 (over y, core).
Axes of the slice: x: 2, y: 2, z: 4, core: 2. Of those that a mesh axis runs over, the one named last changes fastest.
Arguments:
- tokens: bfloat16 [16384, 1152], P(('dp', 'tensor')), may hold values from -6 to 6
- gain_one: float32 [1152], replicated, may hold values from 0.5 to 1.5
- shift_one: float32 [1152], replicated, may hold values from -2 to 2
- w_query: float32 [1152, 1152], P('dp', 'tensor'), may hold values from -0.25 to 0.25
- b_query: float32 [1152], replicated, may hold values from -2 to 2
- w_key: float32 [1152, 1152], P('dp', 'tensor'), may hold values from -0.25 to 0.25
- w_value: float32 [1152, 1152], P('dp', 'tensor'), may hold values from -0.1875 to 0.1875
- b_value: float32 [1152], replicated, may hold values from -2 to 2
- w_out: float32 [1152, 1152], P('tensor', 'dp'), may hold values from -0.75 to 0.75
- b_out: float32 [1152], replicated, may hold values from -2 to 2
- gain_two: float32 [1152], replicated, may hold values from 0.5 to 1.5
- shift_two: float32 [1152], replicated, may hold values from -2 to 2
- w_up: float32 [1152, 4304], P('dp', 'tensor'), may hold values from -0.1875 to 0.1875
- b_up: float32 [4304], replicated, may hold values from -2 to 2
- w_down: float32 [4304, 1152], P('tensor', 'dp'), may hold values from -0.09375 to 0.09375
- b_down: float32 [1152], replicated, may hold values from -2 to 2
- cotangent: bfloat16 [16384, 1152], P(('dp', 'tensor')), may hold values from -6 to 6
Outputs:
- output: bfloat16 [16384, 1152], P(('dp', 'tensor'))
- grad_tokens: bfloat16 [16384, 1152], P(('dp', 'tensor'))
- grad_gain_one: float32 [1152], replicated
- grad_shift_one: float32 [1152], replicated
- grad_w_query: float32 [1152, 1152], P('dp', 'tensor')
- grad_b_query: float32 [1152], replicated
- grad_w_key: float32 [1152, 1152], P('dp', 'tensor')
- grad_w_value: float32 [1152, 1152], P('dp', 'tensor')
- grad_b_value: float32 [1152], replicated
- grad_w_out: float32 [1152, 1152], P('tensor', 'dp')
- grad_b_out: float32 [1152], replicated
- grad_gain_two: float32 [1152], replicated
- grad_shift_two: float32 [1152], replicated
- grad_w_up: float32 [1152, 4304], P('dp', 'tensor')
- grad_b_up: float32 [4304], replicated
- grad_w_down: float32 [4304, 1152], P('tensor', 'dp')
- grad_b_down: float32 [1152], replicated
The draws below stay inside these ranges and needn't reach their ends.
All inputs are finite; a program needn't handle non-finite values.
Results may differ from the reference program's by a relative error of at most 0.02.
Values may be sent and summed in bfloat16 or wider, within the bound.
No kernel may reach another device: no remote copies, remote signals or barrier semaphores. Data moves between devices by JAX's collectives and lax.ppermute only.
A program may use at most 192 MiB of HBM per device.

```python
import jax
import jax.numpy as jnp
from jax import lax

D = 1152
HEADS = 16
HD = 72
FF = 4304
LEN = 1024
IMG_DEV = 2
TOKENS = 16384
N_DP = 8


def steps_of(rng, shape, pieces, least, largest):
    loudness, own = 1.0, jax.random.fold_in(rng, 6)
    for dim, blocks in pieces:
        draws = jnp.exp(jax.random.uniform(jax.random.fold_in(own, dim), (blocks,), jnp.float32, least / len(pieces), largest / len(pieces)))
        loudness = loudness * jnp.repeat(draws, shape[dim] // blocks).reshape([-1 if axis == dim else 1 for axis in range(len(shape))])
    return loudness


def bell_draw(rng, dims, scale, most, shards=(), held_as=jnp.bfloat16):
    entries = scale * jax.random.normal(rng, dims, jnp.float32)
    if shards:
        entries = entries * steps_of(rng, dims, shards, -0.22, 0.18)
    return jnp.clip(entries, -most, most).astype(held_as)


def setup_inputs(seed: int = 0) -> dict:
    streams_of = jax.random.split(jax.random.key(seed), 18)
    return {
        "tokens": bell_draw(streams_of[0], (TOKENS, D), 1.0, 6.0, ((0, 32),)),
        "gain_one": jnp.clip(1.0 + 0.1 * jax.random.normal(streams_of[1], (D,), jnp.float32), 0.5, 1.5),
        "shift_one": bell_draw(streams_of[2], (D,), 0.3, 2.0, (), jnp.float32),
        "w_query": bell_draw(streams_of[3], (D, D), (D // 2) ** -0.5, 0.25, ((0, 8), (1, 4)), jnp.float32),
        "b_query": bell_draw(streams_of[4], (D,), 0.3, 2.0, (), jnp.float32),
        "w_key": bell_draw(streams_of[5], (D, D), (D // 2) ** -0.5, 0.25, ((0, 8), (1, 4)), jnp.float32),
        "w_value": bell_draw(streams_of[6], (D, D), D ** -0.5, 0.1875, ((0, 8), (1, 4)), jnp.float32),
        "b_value": bell_draw(streams_of[7], (D,), 0.3, 2.0, (), jnp.float32),
        "w_out": bell_draw(streams_of[8], (D, D), HD ** -0.5, 0.75, ((0, 4), (1, 8)), jnp.float32),
        "b_out": bell_draw(streams_of[9], (D,), 0.3, 2.0, (), jnp.float32),
        "gain_two": jnp.clip(1.0 + 0.1 * jax.random.normal(streams_of[10], (D,), jnp.float32), 0.5, 1.5),
        "shift_two": bell_draw(streams_of[11], (D,), 0.3, 2.0, (), jnp.float32),
        "w_up": bell_draw(streams_of[12], (D, FF), D ** -0.5, 0.1875, ((0, 8), (1, 4)), jnp.float32),
        "b_up": bell_draw(streams_of[13], (FF,), 0.3, 2.0, (), jnp.float32),
        "w_down": bell_draw(streams_of[14], (FF, D), FF ** -0.5, 0.09375, ((0, 4), (1, 8)), jnp.float32),
        "b_down": bell_draw(streams_of[15], (D,), 0.3, 2.0, (), jnp.float32),
        "cotangent": bell_draw(streams_of[16], (TOKENS, D), 1.0, 6.0, ((0, 32),)),
    }


@jax.custom_vjp
def low(v):
    return lax.optimization_barrier(v.astype(jnp.bfloat16)).astype(jnp.float32)

@jax.custom_vjp
def low_back(v):
    return v

def low_keep(v):
    return (low(v), None)

def low_pass(kept, grad):
    return (grad,)

def back_keep(v):
    return (v, None)

def back_low(kept, grad):
    return (low(grad),)
low.defvjp(low_keep, low_pass)
low_back.defvjp(back_keep, back_low)

def layer_norm(values, norm_gain, norm_shift):
    centred = values - lax.optimization_barrier(jnp.mean(values, axis=-1, keepdims=True))
    spread = lax.optimization_barrier(jnp.mean(centred * centred, axis=-1, keepdims=True))
    return centred * lax.rsqrt(spread + 1e-06) * norm_gain + norm_shift

def product(left, right):
    return jnp.dot(left, right, precision=lax.Precision.HIGHEST, preferred_element_type=jnp.float32)

def attend_image(triple):
    queries, keys_all, values_all = triple
    scores = jnp.einsum('qhd,khd->hqk', queries, keys_all, precision=lax.Precision.HIGHEST) * HD ** (-0.5)
    scores = low_back(scores)
    probs_low = low(jax.nn.softmax(scores, axis=-1))
    return jnp.einsum('hqk,khd->qhd', probs_low, values_all, precision=lax.Precision.HIGHEST)

def block_layer(inputs, gain_one, shift_one, w_query, b_query, w_key, w_value, b_value, w_out, b_out, gain_two, shift_two, w_up, b_up, w_down, b_down):
    row_total = inputs.shape[0]
    images = row_total // LEN
    normed_one = low(layer_norm(inputs, gain_one, shift_one))
    queries = low(low_back(product(normed_one, low(w_query)) + b_query))
    keys_all = low(low_back(product(normed_one, low(w_key))))
    values_all = low(low_back(product(normed_one, low(w_value)) + b_value))

    def per_image(matrix):
        return matrix.reshape(images, LEN, HEADS, HD)
    mixed_low = lax.map(jax.checkpoint(attend_image), (per_image(queries), per_image(keys_all), per_image(values_all)))
    mixed_low = low(low_back(mixed_low.reshape(row_total, D)))
    attention = low_back(product(mixed_low, low(w_out)) + b_out)
    residual = inputs + attention
    normed_two = low(layer_norm(residual, gain_two, shift_two))
    pre_act = low_back(product(normed_two, low(w_up)) + b_up)
    hidden = low(jax.nn.gelu(pre_act, approximate=True))
    return residual + product(hidden, low(w_down)) + b_down

def reference(tokens, gain_one, shift_one, w_query, b_query, w_key, w_value, b_value, w_out, b_out, gain_two, shift_two, w_up, b_up, w_down, b_down, cotangent):
    params = (gain_one, shift_one, w_query, b_query, w_key, w_value, b_value, w_out, b_out, gain_two, shift_two, w_up, b_up, w_down, b_down)
    group_rows = IMG_DEV * LEN
    inputs = tokens.astype(jnp.float32).reshape(N_DP, group_rows, D)
    seeds = cotangent.astype(jnp.float32).reshape(N_DP, group_rows, D)

    def one_group(summed, pair_in):
        block_in, block_seed = pair_in
        block_out, pullback = jax.vjp(block_layer, block_in, *params)
        gradients = pullback(block_seed)
        summed = tuple((older + fresh for older, fresh in zip(summed, gradients[1:])))
        return (summed, (block_out.astype(jnp.bfloat16), gradients[0].astype(jnp.bfloat16)))
    initial = tuple((jnp.zeros_like(param) for param in params))
    summed, (outputs, input_grads) = lax.scan(one_group, initial, (inputs, seeds))
    return (outputs.reshape(TOKENS, D), input_grads.reshape(TOKENS, D), summed[0], summed[1], summed[2], summed[3], summed[4], summed[5], summed[6], summed[7], summed[8], summed[9], summed[10], summed[11], summed[12], summed[13], summed[14])
```

```python
import functools
import math

import jax
import jax.numpy as jnp
from jax import lax
from jax.experimental import pallas as pl
from jax.experimental.pallas import tpu as pltpu
from jax.sharding import PartitionSpec as P

HD = 72
LEN = 1024
NORM_EPS = 1e-06
LOW = jnp.bfloat16
F32 = jnp.float32
SCALE = HD ** (-0.5)
SCALE_LOG2 = SCALE * math.log2(math.e)
VMEM_LIMIT = 50 * 1024 * 1024

NN = (((1,), (0,)), ((), ()))
NT = (((1,), (1,)), ((), ()))
TN = (((0,), (0,)), ((), ()))


def dot(left, right, dims=NN):
    return lax.dot_general(left, right, dims, preferred_element_type=F32)


def layer_norm(values, norm_gain, norm_shift):
    centred = values - jnp.mean(values, axis=-1, keepdims=True)
    spread = jnp.mean(centred * centred, axis=-1, keepdims=True)
    return centred * lax.rsqrt(spread + NORM_EPS) * norm_gain + norm_shift


def gelu_tanh(values):
    return jax.nn.gelu(values, approximate=True)


def attend_forward_body(heads, block, qkv_ref, mixed_ref, lse_ref, q_s, k_s, vt_s, ot_s):
    cols = heads * HD
    for h in range(heads):
        lo = h * HD
        q_s[...] = qkv_ref[:, lo : lo + HD]
        k_s[...] = qkv_ref[:, cols + lo : cols + lo + HD]
        vt_s[...] = qkv_ref[:, 2 * cols + lo : 2 * cols + lo + HD].T

        def one_block(j, carry):
            at = pl.ds(pl.multiple_of(j * block, block), block)
            scores = dot(k_s[...], q_s[at, :], NT)
            highest = jnp.max(scores, axis=0, keepdims=True)
            probs = jnp.exp2((scores - highest) * SCALE_LOG2)
            total = jnp.sum(probs, axis=0, keepdims=True)
            mixed = dot(vt_s[...], probs.astype(LOW))
            ot_s[:, at] = mixed / total
            lse_ref[h : h + 1, at] = highest * SCALE_LOG2 + jnp.log2(total)
            return carry

        lax.fori_loop(0, LEN // block, one_block, 0)
        mixed_ref[:, lo : lo + HD] = ot_s[...].T.astype(LOW)


def attend_forward(qkv, heads):
    images, rows, _ = qkv.shape
    cols = heads * HD
    block = 256
    return pl.pallas_call(
        functools.partial(attend_forward_body, heads, block),
        grid=(images,),
        in_specs=[pl.BlockSpec((None, rows, 3 * cols), lambda i: (i, 0, 0))],
        out_specs=[
            pl.BlockSpec((None, rows, cols), lambda i: (i, 0, 0)),
            pl.BlockSpec((None, heads, rows), lambda i: (i, 0, 0)),
        ],
        out_shape=[
            jax.ShapeDtypeStruct((images, rows, cols), LOW),
            jax.ShapeDtypeStruct((images, heads, rows), F32),
        ],
        scratch_shapes=[
            pltpu.VMEM((rows, HD), LOW),
            pltpu.VMEM((rows, HD), LOW),
            pltpu.VMEM((HD, rows), LOW),
            pltpu.VMEM((HD, rows), F32),
        ],
        compiler_params=pltpu.CompilerParams(vmem_limit_bytes=VMEM_LIMIT),
        cost_estimate=pl.CostEstimate(
            flops=images * heads * rows * rows * 1024,
            bytes_accessed=images * rows * cols * 8,
            transcendentals=images * heads * rows * rows,
        ),
        name="attend_forward",
    )(qkv)


def attend_backward_body(
    heads, block, qkv_ref, grad_ref, mixed_ref, lse_ref, out_ref, q_s, k_s, v_s, do_s, kt_s, dqt_s, dk_s, dv_s, delta_s
):
    cols = heads * HD
    for h in range(heads):
        lo = h * HD
        q_s[...] = qkv_ref[:, lo : lo + HD]
        keys = qkv_ref[:, cols + lo : cols + lo + HD]
        k_s[...] = keys
        kt_s[...] = keys.T
        v_s[...] = qkv_ref[:, 2 * cols + lo : 2 * cols + lo + HD]
        grads = grad_ref[:, lo : lo + HD]
        do_s[...] = grads
        products = grads.astype(F32) * mixed_ref[:, lo : lo + HD].astype(F32)
        delta_s[...] = jnp.sum(products.T, axis=0, keepdims=True)
        dk_s[...] = jnp.zeros_like(dk_s)
        dv_s[...] = jnp.zeros_like(dv_s)

        def one_block(j, carry):
            at = pl.ds(pl.multiple_of(j * block, block), block)
            query = q_s[at, :]
            grad = do_s[at, :]
            scores = dot(k_s[...], query, NT)
            probs = jnp.exp2(scores * SCALE_LOG2 - lse_ref[h : h + 1, at])
            prob_grad = dot(v_s[...], grad, NT)
            dv_s[...] += dot(probs.astype(LOW), grad)
            score_grad = (probs * (prob_grad - delta_s[:, at])).astype(LOW)
            dk_s[...] += dot(score_grad, query)
            dqt_s[:, at] = dot(kt_s[...], score_grad)
            return carry

        lax.fori_loop(0, LEN // block, one_block, 0)
        out_ref[:, lo : lo + HD] = (dqt_s[...] * SCALE).T.astype(LOW)
        out_ref[:, cols + lo : cols + lo + HD] = (dk_s[...] * SCALE).astype(LOW)
        out_ref[:, 2 * cols + lo : 2 * cols + lo + HD] = dv_s[...].astype(LOW)


def attend_backward(qkv, grads, mixed, lse, heads):
    images, rows, _ = qkv.shape
    cols = heads * HD
    block = 256
    return pl.pallas_call(
        functools.partial(attend_backward_body, heads, block),
        grid=(images,),
        in_specs=[
            pl.BlockSpec((None, rows, 3 * cols), lambda i: (i, 0, 0)),
            pl.BlockSpec((None, rows, cols), lambda i: (i, 0, 0)),
            pl.BlockSpec((None, rows, cols), lambda i: (i, 0, 0)),
            pl.BlockSpec((None, heads, rows), lambda i: (i, 0, 0)),
        ],
        out_specs=pl.BlockSpec((None, rows, 3 * cols), lambda i: (i, 0, 0)),
        out_shape=jax.ShapeDtypeStruct((images, rows, 3 * cols), LOW),
        scratch_shapes=[
            pltpu.VMEM((rows, HD), LOW),
            pltpu.VMEM((rows, HD), LOW),
            pltpu.VMEM((rows, HD), LOW),
            pltpu.VMEM((rows, HD), LOW),
            pltpu.VMEM((HD, rows), LOW),
            pltpu.VMEM((HD, rows), F32),
            pltpu.VMEM((rows, HD), F32),
            pltpu.VMEM((rows, HD), F32),
            pltpu.VMEM((1, rows), F32),
        ],
        compiler_params=pltpu.CompilerParams(vmem_limit_bytes=VMEM_LIMIT),
        cost_estimate=pl.CostEstimate(
            flops=images * heads * rows * rows * 2560,
            bytes_accessed=images * rows * cols * 18,
            transcendentals=images * heads * rows * rows,
        ),
        name="attend_backward",
    )(qkv, grads, mixed, lse)


def place_body(count, first, table_ref, *refs):
    sources, out_ref, sem = refs[:-2], refs[-2], refs[-1]

    def piece(start, n):
        slot = table_ref[n]
        for at, source in enumerate(sources):
            @pl.when((slot >= at * first) & (slot < (at + 1) * first))
            def _():
                copy = pltpu.make_async_copy(source.at[slot - at * first], out_ref.at[n], sem.at[n])
                if start:
                    copy.start()
                else:
                    copy.wait()

    for n in range(count):
        piece(True, n)
    for n in range(count):
        piece(False, n)


def place(table, sources, name):
    first, *shape = sources[0].shape
    count = table.shape[0]
    if shape[0] % 16:
        return jnp.take(jnp.concatenate(sources, axis=0), table, axis=0)
    return pl.pallas_call(
        functools.partial(place_body, count, first),
        in_specs=[pl.BlockSpec(memory_space=pltpu.SMEM)] + [pl.BlockSpec(memory_space=pl.ANY)] * len(sources),
        out_specs=pl.BlockSpec(memory_space=pl.ANY),
        out_shape=jax.ShapeDtypeStruct((count, *shape), LOW),
        scratch_shapes=[pltpu.SemaphoreType.DMA((count,))],
        name=name,
    )(table, *sources)


class Plan:
    def __init__(self, n_dp, n_t, ranks):
        self.n_dp, self.n_t, self.ranks = n_dp, n_t, ranks
        self.images = n_t // ranks
        dims = [("dp", 1 << b) for b in reversed(range(n_dp.bit_length() - 1))]
        image_dims = [("image", 1 << b) for b in reversed(range(self.images.bit_length() - 1))]
        even = dims + image_dims
        odd = list(even)
        if image_dims and dims:
            odd[-2], odd[-1] = odd[-1], odd[-2]
        self.orders = (even, odd)
        self.stages = len(even)
        self.rank_stages = ranks.bit_length() - 1

    def permute(self, values, partner):
        pairs = []
        for d in range(self.n_dp):
            for t in range(self.n_t):
                d2, i2, r2 = partner(d, t // self.ranks, t % self.ranks)
                pairs.append((d * self.n_t + t, d2 * self.n_t + i2 * self.ranks + r2))
        return lax.ppermute(values, ("dp", "tensor"), pairs)

    def exchange(self, values, stage):
        def partner(d, i, r):
            kind, step = self.orders[r & 1][stage]
            return (d ^ step, i, r) if kind == "dp" else (d, i ^ step, r)

        return self.permute(values, partner)

    def rank_exchange(self, values, stage):
        return self.permute(values, lambda d, i, r: (d, i, r ^ (1 << stage)))

    def slots(self):
        me_dp, me_t = lax.axis_index("dp"), lax.axis_index("tensor")
        flips = jnp.arange(self.n_dp, dtype=jnp.int32)[None, :] ^ me_dp
        images = jnp.arange(self.images, dtype=jnp.int32)[:, None]

        def table(order):
            total = jnp.zeros((self.images, self.n_dp), jnp.int32)
            for stage, (kind, step) in enumerate(order):
                source = flips if kind == "dp" else images
                total = total + jnp.where((source & step) != 0, 1 << stage, 0)
            return total

        return jnp.where((me_t % self.ranks) & 1, table(self.orders[1]), table(self.orders[0]))

    def gather(self, shard):
        mine = shard[None]
        for stage in range(self.stages):
            theirs = self.exchange(mine, stage)
            if stage == self.stages - 1:
                return (mine, theirs)
            mine = jnp.concatenate([mine, theirs], axis=0)
        return (mine,)

    def scatter(self, pieces):
        for stage in reversed(range(self.stages)):
            half = pieces.shape[0] // 2
            theirs = self.exchange(pieces[half:], stage)
            total = pieces[:half].astype(F32) + theirs.astype(F32)
            pieces = total if stage == 0 else total.astype(LOW)
        return pieces[0]

    def rank_gather(self, shard):
        mine = shard
        for stage in range(self.rank_stages):
            mine = jnp.concatenate([mine, self.rank_exchange(mine, stage)], axis=0)
        return mine

    def rank_scatter(self, rows):
        for stage in reversed(range(self.rank_stages)):
            half = rows.shape[0] // 2
            theirs = self.rank_exchange(rows[half:].astype(LOW), stage)
            rows = rows[:half] + theirs.astype(F32)
        return rows


def local(
    tokens, gain_one, shift_one, w_query, b_query, w_key, w_value, b_value, w_out, b_out,
    gain_two, shift_two, w_up, b_up, w_down, b_down, cotangent, plan=None,
):
    images, ranks, n_dp = plan.images, plan.ranks, plan.n_dp
    shard_rows = w_query.shape[0]
    width = tokens.shape[1]
    head_cols, hidden_cols = w_query.shape[1], w_up.shape[1]
    heads = head_cols // HD
    me_t = lax.axis_index("tensor")
    me_image, me_rank = me_t // ranks, me_t % ranks
    slot_table = plan.slots().reshape(-1)
    piece_table = jnp.zeros_like(slot_table).at[slot_table].set(jnp.arange(slot_table.shape[0], dtype=jnp.int32))

    def shard_of(i):
        return (me_image ^ i) * ranks + me_rank

    def columns(vector, cols):
        return jnp.stack([lax.dynamic_slice_in_dim(vector, shard_of(i) * cols, cols) for i in range(images)])

    def uncolumns(parts, length):
        cols = parts.shape[1]
        blank = jnp.zeros((length,), F32)
        for i in range(images):
            blank = lax.dynamic_update_slice_in_dim(blank, parts[i], shard_of(i) * cols, 0)
        return blank

    def gathered(shard, name):
        full = place(slot_table, plan.gather(shard), name)
        return full.reshape(images, n_dp * shard_rows, shard.shape[1])

    def scattered(grads, name):
        pieces = jnp.concatenate(grads, axis=0).reshape(images * n_dp, shard_rows, -1)
        return plan.scatter(place(piece_table, [pieces], name))

    low = lambda v: v.astype(LOW)
    qkv_full = gathered(jnp.concatenate([low(w_query), low(w_key), low(w_value)], axis=1), "place_qkv")
    out_full = gathered(low(w_out).T, "place_out")
    up_full = gathered(low(w_up), "place_up")
    down_full = gathered(low(w_down).T, "place_down")

    cot_rows = plan.rank_gather(cotangent)
    inputs32 = tokens.astype(F32)
    normed_one = layer_norm(inputs32, gain_one, shift_one).astype(LOW)
    rows_one = plan.rank_gather(normed_one)
    qkv_bias = jnp.concatenate(
        [columns(b_query, head_cols), jnp.zeros((images, head_cols), F32), columns(b_value, head_cols)], axis=1
    )
    qkv = jnp.stack([low(dot(rows_one, qkv_full[i]) + qkv_bias[i]) for i in range(images)])
    mixed, lse = attend_forward(qkv, heads)

    attn = sum(dot(mixed[i], out_full[i], NT) for i in range(images))
    residual = inputs32 + plan.rank_scatter(attn) + b_out
    normed_two = layer_norm(residual, gain_two, shift_two).astype(LOW)
    rows_two = plan.rank_gather(normed_two)
    up_bias = columns(b_up, hidden_cols)
    pre_act, act = [], []
    for i in range(images):
        pre_act.append(dot(rows_two, up_full[i]) + up_bias[i])
        act.append(low(gelu_tanh(pre_act[i])))
    mlp = sum(dot(act[i], down_full[i], NT) for i in range(images))
    output = low(residual + plan.rank_scatter(mlp) + b_down)

    grad_out = cotangent.astype(F32)
    down_bias_grad = jnp.sum(grad_out, axis=0)
    pre_low, down_grads, up_grads, up_bias_parts = [], [], [], []
    for i in range(images):
        down_grads.append(low(dot(cot_rows, act[i], TN)))
        act_grad = dot(cot_rows, down_full[i])
        _, pull = jax.vjp(gelu_tanh, pre_act[i])
        pre_low.append(low(pull(act_grad)[0]))
        up_bias_parts.append(jnp.sum(pre_low[i], axis=0, dtype=F32))
        up_grads.append(low(dot(rows_two, pre_low[i], TN)))
    down_grad = scattered(down_grads, "place_grad_down").T
    up_grad = scattered(up_grads, "place_grad_up")
    up_bias_grad = uncolumns(jnp.stack(up_bias_parts), b_up.shape[0])
    norm_two_grad = plan.rank_scatter(sum(dot(pre_low[i], up_full[i], NT) for i in range(images)))
    _, pull_two = jax.vjp(layer_norm, residual, gain_two, shift_two)
    residual_part, gain_two_grad, shift_two_grad = pull_two(norm_two_grad)
    residual_grad = grad_out + residual_part
    branch_low = low(residual_grad)
    out_bias_grad = jnp.sum(branch_low, axis=0, dtype=F32)
    branch_rows = plan.rank_gather(branch_low)

    mixed_grad = jnp.stack([low(dot(branch_rows, out_full[i])) for i in range(images)])
    out_grad = scattered([low(dot(branch_rows, mixed[i], TN)) for i in range(images)], "place_grad_out").T
    qkv_grads = attend_backward(qkv, mixed_grad, mixed, lse, heads)
    qkv_grad = scattered([low(dot(rows_one, qkv_grads[i], TN)) for i in range(images)], "place_grad_qkv")
    query_grad, key_grad, value_grad = (qkv_grad[:, n * head_cols : (n + 1) * head_cols] for n in range(3))
    qkv_sums = jnp.sum(qkv_grads, axis=1, dtype=F32)
    query_bias_grad = uncolumns(qkv_sums[:, :head_cols], b_query.shape[0])
    value_bias_grad = uncolumns(qkv_sums[:, 2 * head_cols :], b_value.shape[0])
    norm_one_grad = plan.rank_scatter(sum(dot(qkv_grads[i], qkv_full[i], NT) for i in range(images)))
    _, pull_one = jax.vjp(layer_norm, inputs32, gain_one, shift_one)
    input_part, gain_one_grad, shift_one_grad = pull_one(norm_one_grad)
    grad_tokens = low(residual_grad + input_part)

    small = lax.psum(
        (
            gain_one_grad, shift_one_grad, query_bias_grad, value_bias_grad, out_bias_grad,
            gain_two_grad, shift_two_grad, up_bias_grad, down_bias_grad,
        ),
        ("dp", "tensor"),
    )
    return (
        output, grad_tokens, small[0], small[1], query_grad, small[2], key_grad, value_grad, small[3],
        out_grad, small[4], small[5], small[6], up_grad, small[7], down_grad, small[8],
    )


def solution(mesh):
    split = P(("dp", "tensor"), None)
    whole, wide, tall = P(), P("dp", "tensor"), P("tensor", "dp")
    n_dp, n_t = mesh.shape["dp"], mesh.shape["tensor"]

    def layer(*args):
        rows = args[0].shape[0] // (n_dp * n_t)
        plan = Plan(n_dp, n_t, LEN // rows)
        return jax.shard_map(
            functools.partial(local, plan=plan),
            mesh=mesh,
            in_specs=(
                split, whole, whole, wide, whole, wide, wide, whole, tall, whole,
                whole, whole, wide, whole, tall, whole, split,
            ),
            out_specs=(
                split, split, whole, whole, wide, whole, wide, wide, whole,
                tall, whole, whole, whole, wide, whole, tall, whole,
            ),
            check_vma=False,
        )(*args)

    return layer
```

```python
import functools
import math

import jax
import jax.numpy as jnp
from jax import lax
from jax.experimental import pallas as pl
from jax.experimental.pallas import tpu as pltpu
from jax.sharding import PartitionSpec as P

HD = 72
LEN = 1024
NORM_EPS = 1e-06
LOW = jnp.bfloat16
F32 = jnp.float32
SCALE = HD ** (-0.5)
SCALE_LOG2 = SCALE * math.log2(math.e)
VMEM_LIMIT = 50 * 1024 * 1024

NN = (((1,), (0,)), ((), ()))
NT = (((1,), (1,)), ((), ()))
TN = (((0,), (0,)), ((), ()))


def dot(left, right, dims=NN):
    return lax.dot_general(left, right, dims, preferred_element_type=F32)


def layer_norm(values, norm_gain, norm_shift):
    centred = values - jnp.mean(values, axis=-1, keepdims=True)
    spread = jnp.mean(centred * centred, axis=-1, keepdims=True)
    return centred * lax.rsqrt(spread + NORM_EPS) * norm_gain + norm_shift


def gelu_tanh(values):
    return jax.nn.gelu(values, approximate=True)


def attend_forward_body(heads, qkv_ref, mixed_ref, lse_ref):
    cols = heads * HD
    for h in range(heads):
        lo = h * HD
        queries = qkv_ref[:, lo : lo + HD]
        keys = qkv_ref[:, cols + lo : cols + lo + HD]
        values = qkv_ref[:, 2 * cols + lo : 2 * cols + lo + HD]
        scores = dot(keys, queries, NT)
        highest = jnp.max(scores, axis=0, keepdims=True)
        probs = jnp.exp2((scores - highest) * SCALE_LOG2)
        total = jnp.sum(probs, axis=0, keepdims=True)
        mixed = dot(values.T, probs.astype(LOW)) / total
        lse_ref[h : h + 1, :] = highest * SCALE_LOG2 + jnp.log2(total)
        mixed_ref[:, lo : lo + HD] = mixed.T.astype(LOW)


def attend_forward(qkv, heads):
    images, rows, _ = qkv.shape
    cols = heads * HD
    return pl.pallas_call(
        functools.partial(attend_forward_body, heads),
        grid=(images,),
        in_specs=[pl.BlockSpec((None, rows, 3 * cols), lambda i: (i, 0, 0))],
        out_specs=[
            pl.BlockSpec((None, rows, cols), lambda i: (i, 0, 0)),
            pl.BlockSpec((None, heads, rows), lambda i: (i, 0, 0)),
        ],
        out_shape=[
            jax.ShapeDtypeStruct((images, rows, cols), LOW),
            jax.ShapeDtypeStruct((images, heads, rows), F32),
        ],
        compiler_params=pltpu.CompilerParams(vmem_limit_bytes=VMEM_LIMIT),
        cost_estimate=pl.CostEstimate(
            flops=images * heads * rows * rows * 2048,
            bytes_accessed=images * rows * cols * 8,
            transcendentals=images * heads * rows * rows,
        ),
        name="attend_forward",
    )(qkv)


def attend_backward_body(heads, qkv_ref, grad_ref, mixed_ref, lse_ref, out_ref):
    cols = heads * HD
    for h in range(heads):
        lo = h * HD
        queries = qkv_ref[:, lo : lo + HD]
        keys = qkv_ref[:, cols + lo : cols + lo + HD]
        values = qkv_ref[:, 2 * cols + lo : 2 * cols + lo + HD]
        grads = grad_ref[:, lo : lo + HD]
        products = grads.astype(F32) * mixed_ref[:, lo : lo + HD].astype(F32)
        delta = jnp.sum(products.T, axis=0, keepdims=True)
        probs = jnp.exp2(dot(keys, queries, NT) * SCALE_LOG2 - lse_ref[h : h + 1, :])
        prob_grad = dot(values, grads, NT)
        out_ref[:, 2 * cols + lo : 2 * cols + lo + HD] = dot(probs.astype(LOW), grads).astype(LOW)
        score_grad = (probs * (prob_grad - delta)).astype(LOW)
        out_ref[:, cols + lo : cols + lo + HD] = (dot(score_grad, queries) * SCALE).astype(LOW)
        out_ref[:, lo : lo + HD] = (dot(keys.T, score_grad) * SCALE).T.astype(LOW)


def attend_backward(qkv, grads, mixed, lse, heads):
    images, rows, _ = qkv.shape
    cols = heads * HD
    return pl.pallas_call(
        functools.partial(attend_backward_body, heads),
        grid=(images,),
        in_specs=[
            pl.BlockSpec((None, rows, 3 * cols), lambda i: (i, 0, 0)),
            pl.BlockSpec((None, rows, cols), lambda i: (i, 0, 0)),
            pl.BlockSpec((None, rows, cols), lambda i: (i, 0, 0)),
            pl.BlockSpec((None, heads, rows), lambda i: (i, 0, 0)),
        ],
        out_specs=pl.BlockSpec((None, rows, 3 * cols), lambda i: (i, 0, 0)),
        out_shape=jax.ShapeDtypeStruct((images, rows, 3 * cols), LOW),
        compiler_params=pltpu.CompilerParams(vmem_limit_bytes=VMEM_LIMIT),
        cost_estimate=pl.CostEstimate(
            flops=images * heads * rows * rows * 4096,
            bytes_accessed=images * rows * cols * 18,
            transcendentals=images * heads * rows * rows,
        ),
        name="attend_backward",
    )(qkv, grads, mixed, lse)


def place_body(count, first, table_ref, *refs):
    sources, out_ref, sem = refs[:-2], refs[-2], refs[-1]

    def piece(start, n):
        slot = table_ref[n]
        for at, source in enumerate(sources):
            @pl.when((slot >= at * first) & (slot < (at + 1) * first))
            def _():
                copy = pltpu.make_async_copy(source.at[slot - at * first], out_ref.at[n], sem.at[n])
                if start:
                    copy.start()
                else:
                    copy.wait()

    for n in range(count):
        piece(True, n)
    for n in range(count):
        piece(False, n)


def place(table, sources, name):
    first, *shape = sources[0].shape
    count = table.shape[0]
    if shape[0] % 16:
        return jnp.take(jnp.concatenate(sources, axis=0), table, axis=0)
    size = count * shape[0] * shape[1]
    return pl.pallas_call(
        functools.partial(place_body, count, first),
        in_specs=[pl.BlockSpec(memory_space=pltpu.SMEM)] + [pl.BlockSpec(memory_space=pl.ANY)] * len(sources),
        out_specs=pl.BlockSpec(memory_space=pltpu.VMEM),
        out_shape=jax.ShapeDtypeStruct((count, *shape), LOW),
        scratch_shapes=[pltpu.SemaphoreType.DMA((count,))],
        compiler_params=pltpu.CompilerParams(vmem_limit_bytes=VMEM_LIMIT),
        cost_estimate=pl.CostEstimate(flops=0, bytes_accessed=4 * size, transcendentals=0),
        name=name,
    )(table, *sources)


def weight_grad_body(images, n_dp, half, table_ref, left_ref, *refs):
    rights, (keep_ref, send_ref, turned, product, sem) = refs[:images], refs[images:]
    width = turned.shape[0]
    shard_rows = width // n_dp
    turned[...] = left_ref[...].T
    step = width // 2

    def piece(start, n):
        slot = table_ref[n]
        source = product.at[n // n_dp, pl.ds((n % n_dp) * shard_rows, shard_rows)]
        for out_ref, mine, index in ((keep_ref, slot < half, slot), (send_ref, slot >= half, slot - half)):
            @pl.when(mine)
            def _():
                copy = pltpu.make_async_copy(source, out_ref.at[index], sem.at[n])
                if start:
                    copy.start()
                else:
                    copy.wait()

    for i in range(images):
        for part in range(2):
            at = pl.ds(part * step, step)
            product[i, at, :] = dot(turned[at, :], rights[i][...]).astype(LOW)
            for d in range(part * n_dp // 2, (part + 1) * n_dp // 2):
                piece(True, i * n_dp + d)
    for n in range(images * n_dp):
        piece(False, n)


def weight_grad(table, left, rights, n_dp, name):
    images = len(rights)
    rows, width = left.shape
    cols = rights[0].shape[1]
    shard_rows = width // n_dp
    half = images * n_dp // 2
    if shard_rows % 16:
        whole = jnp.concatenate([dot(left, right, TN).astype(LOW) for right in rights], axis=0)
        slots = whole.reshape(images * n_dp, shard_rows, cols)
        order = jnp.zeros_like(table).at[table].set(jnp.arange(table.shape[0], dtype=jnp.int32))
        slots = jnp.take(slots, order, axis=0)
        return slots[:half], slots[half:]
    shape = jax.ShapeDtypeStruct((half, shard_rows, cols), LOW)
    return pl.pallas_call(
        functools.partial(weight_grad_body, images, n_dp, half),
        in_specs=[pl.BlockSpec(memory_space=pltpu.SMEM)] + [pl.BlockSpec(memory_space=pltpu.VMEM)] * (1 + images),
        out_specs=[pl.BlockSpec(memory_space=pl.ANY)] * 2,
        out_shape=[shape, shape],
        scratch_shapes=[
            pltpu.VMEM((width, rows), LOW),
            pltpu.VMEM((images, width, cols), LOW),
            pltpu.SemaphoreType.DMA((images * n_dp,)),
        ],
        compiler_params=pltpu.CompilerParams(vmem_limit_bytes=VMEM_LIMIT),
        cost_estimate=pl.CostEstimate(
            flops=2 * images * rows * width * cols,
            bytes_accessed=2 * (rows * width + images * (rows + width) * cols),
            transcendentals=0,
        ),
        name=name,
    )(table, left, *rights)


class Plan:
    def __init__(self, n_dp, n_t, ranks):
        self.n_dp, self.n_t, self.ranks = n_dp, n_t, ranks
        self.images = n_t // ranks
        dims = [("dp", 1 << b) for b in reversed(range(n_dp.bit_length() - 1))]
        image_dims = [("image", 1 << b) for b in reversed(range(self.images.bit_length() - 1))]
        even = dims + image_dims
        odd = list(even)
        if image_dims and dims:
            odd[-2], odd[-1] = odd[-1], odd[-2]
        self.orders = (even, odd)
        self.stages = len(even)
        self.rank_stages = ranks.bit_length() - 1

    def permute(self, values, partner):
        pairs = []
        for d in range(self.n_dp):
            for t in range(self.n_t):
                d2, i2, r2 = partner(d, t // self.ranks, t % self.ranks)
                pairs.append((d * self.n_t + t, d2 * self.n_t + i2 * self.ranks + r2))
        return lax.ppermute(values, ("dp", "tensor"), pairs)

    def exchange(self, values, stage):
        def partner(d, i, r):
            kind, step = self.orders[r & 1][stage]
            return (d ^ step, i, r) if kind == "dp" else (d, i ^ step, r)

        return self.permute(values, partner)

    def rank_exchange(self, values, stage):
        return self.permute(values, lambda d, i, r: (d, i, r ^ (1 << stage)))

    def slots(self):
        me_dp, me_t = lax.axis_index("dp"), lax.axis_index("tensor")
        flips = jnp.arange(self.n_dp, dtype=jnp.int32)[None, :] ^ me_dp
        images = jnp.arange(self.images, dtype=jnp.int32)[:, None]

        def table(order):
            total = jnp.zeros((self.images, self.n_dp), jnp.int32)
            for stage, (kind, step) in enumerate(order):
                source = flips if kind == "dp" else images
                total = total + jnp.where((source & step) != 0, 1 << stage, 0)
            return total

        return jnp.where((me_t % self.ranks) & 1, table(self.orders[1]), table(self.orders[0]))

    def gather(self, shard):
        mine = shard[None]
        for stage in range(self.stages):
            theirs = self.exchange(mine, stage)
            if stage == self.stages - 1:
                return (mine, theirs)
            mine = jnp.concatenate([mine, theirs], axis=0)
        return (mine,)

    def scatter(self, keep, send):
        for stage in reversed(range(self.stages)):
            theirs = self.exchange(send, stage)
            half = keep.shape[0] // 2
            if stage == 0:
                return (keep.astype(F32) + theirs.astype(F32))[0]
            send = (keep[half:].astype(F32) + theirs[half:].astype(F32)).astype(LOW)
            keep = (keep[:half].astype(F32) + theirs[:half].astype(F32)).astype(LOW)

    def rank_gather(self, shard):
        mine = shard
        for stage in range(self.rank_stages):
            mine = jnp.concatenate([mine, self.rank_exchange(mine, stage)], axis=0)
        return mine

    def rank_scatter(self, rows):
        for stage in reversed(range(self.rank_stages)):
            half = rows.shape[0] // 2
            theirs = self.rank_exchange(rows[half:].astype(LOW), stage)
            rows = rows[:half] + theirs.astype(F32)
        return rows


def local(
    tokens, gain_one, shift_one, w_query, b_query, w_key, w_value, b_value, w_out, b_out,
    gain_two, shift_two, w_up, b_up, w_down, b_down, cotangent, plan=None,
):
    images, ranks, n_dp = plan.images, plan.ranks, plan.n_dp
    shard_rows = w_query.shape[0]
    width = tokens.shape[1]
    head_cols, hidden_cols = w_query.shape[1], w_up.shape[1]
    heads = head_cols // HD
    me_t = lax.axis_index("tensor")
    me_image, me_rank = me_t // ranks, me_t % ranks
    slot_table = plan.slots().reshape(-1)

    def shard_of(i):
        return (me_image ^ i) * ranks + me_rank

    def columns(vector, cols):
        return jnp.stack([lax.dynamic_slice_in_dim(vector, shard_of(i) * cols, cols) for i in range(images)])

    def uncolumns(parts, length):
        cols = parts.shape[1]
        blank = jnp.zeros((length,), F32)
        for i in range(images):
            blank = lax.dynamic_update_slice_in_dim(blank, parts[i], shard_of(i) * cols, 0)
        return blank

    def gathered(shard, name):
        full = place(slot_table, plan.gather(shard), name)
        return full.reshape(images, n_dp * shard_rows, shard.shape[1])

    def scattered(left, rights, name):
        return plan.scatter(*weight_grad(slot_table, left, rights, n_dp, name))

    low = lambda v: v.astype(LOW)
    qkv_full = gathered(jnp.concatenate([low(w_query), low(w_key), low(w_value)], axis=1), "place_qkv")
    out_full = gathered(low(w_out).T, "place_out")
    up_full = gathered(low(w_up), "place_up")
    down_full = gathered(low(w_down).T, "place_down")

    cot_rows = plan.rank_gather(cotangent)
    inputs32 = tokens.astype(F32)
    normed_one = layer_norm(inputs32, gain_one, shift_one).astype(LOW)
    rows_one = plan.rank_gather(normed_one)
    qkv_bias = jnp.concatenate(
        [columns(b_query, head_cols), jnp.zeros((images, head_cols), F32), columns(b_value, head_cols)], axis=1
    )
    qkv = jnp.stack([low(dot(rows_one, qkv_full[i]) + qkv_bias[i]) for i in range(images)])
    mixed, lse = attend_forward(qkv, heads)

    attn = sum(dot(mixed[i], out_full[i], NT) for i in range(images))
    residual = inputs32 + plan.rank_scatter(attn) + b_out
    normed_two = layer_norm(residual, gain_two, shift_two).astype(LOW)
    rows_two = plan.rank_gather(normed_two)
    up_bias = columns(b_up, hidden_cols)
    pre_act, act = [], []
    for i in range(images):
        pre_act.append(dot(rows_two, up_full[i]) + up_bias[i])
        act.append(low(gelu_tanh(pre_act[i])))
    mlp = sum(dot(act[i], down_full[i], NT) for i in range(images))
    output = low(residual + plan.rank_scatter(mlp) + b_down)

    grad_out = cotangent.astype(F32)
    down_bias_grad = jnp.sum(grad_out, axis=0)
    pre_low, up_bias_parts = [], []
    for i in range(images):
        act_grad = dot(cot_rows, down_full[i])
        _, pull = jax.vjp(gelu_tanh, pre_act[i])
        pre_low.append(low(pull(act_grad)[0]))
        up_bias_parts.append(jnp.sum(pre_low[i], axis=0, dtype=F32))
    down_grad = scattered(cot_rows, act, "grad_down").T
    up_grad = scattered(rows_two, pre_low, "grad_up")
    up_bias_grad = uncolumns(jnp.stack(up_bias_parts), b_up.shape[0])
    norm_two_grad = plan.rank_scatter(sum(dot(pre_low[i], up_full[i], NT) for i in range(images)))
    _, pull_two = jax.vjp(layer_norm, residual, gain_two, shift_two)
    residual_part, gain_two_grad, shift_two_grad = pull_two(norm_two_grad)
    residual_grad = grad_out + residual_part
    branch_low = low(residual_grad)
    out_bias_grad = jnp.sum(branch_low, axis=0, dtype=F32)
    branch_rows = plan.rank_gather(branch_low)

    mixed_grad = jnp.stack([low(dot(branch_rows, out_full[i])) for i in range(images)])
    out_grad = scattered(branch_rows, list(mixed), "grad_out").T
    qkv_grads = attend_backward(qkv, mixed_grad, mixed, lse, heads)
    qkv_grad = scattered(rows_one, list(qkv_grads), "grad_qkv")
    query_grad, key_grad, value_grad = (qkv_grad[:, n * head_cols : (n + 1) * head_cols] for n in range(3))
    qkv_sums = jnp.sum(qkv_grads, axis=1, dtype=F32)
    query_bias_grad = uncolumns(qkv_sums[:, :head_cols], b_query.shape[0])
    value_bias_grad = uncolumns(qkv_sums[:, 2 * head_cols :], b_value.shape[0])
    norm_one_grad = plan.rank_scatter(sum(dot(qkv_grads[i], qkv_full[i], NT) for i in range(images)))
    _, pull_one = jax.vjp(layer_norm, inputs32, gain_one, shift_one)
    input_part, gain_one_grad, shift_one_grad = pull_one(norm_one_grad)
    grad_tokens = low(residual_grad + input_part)

    small = lax.psum(
        (
            gain_one_grad, shift_one_grad, query_bias_grad, value_bias_grad, out_bias_grad,
            gain_two_grad, shift_two_grad, up_bias_grad, down_bias_grad,
        ),
        ("dp", "tensor"),
    )
    return (
        output, grad_tokens, small[0], small[1], query_grad, small[2], key_grad, value_grad, small[3],
        out_grad, small[4], small[5], small[6], up_grad, small[7], down_grad, small[8],
    )


def solution(mesh):
    split = P(("dp", "tensor"), None)
    whole, wide, tall = P(), P("dp", "tensor"), P("tensor", "dp")
    n_dp, n_t = mesh.shape["dp"], mesh.shape["tensor"]

    def layer(*args):
        rows = args[0].shape[0] // (n_dp * n_t)
        plan = Plan(n_dp, n_t, LEN // rows)
        return jax.shard_map(
            functools.partial(local, plan=plan),
            mesh=mesh,
            in_specs=(
                split, whole, whole, wide, whole, wide, wide, whole, tall, whole,
                whole, whole, wide, whole, tall, whole, split,
            ),
            out_specs=(
                split, split, whole, whole, wide, whole, wide, wide, whole,
                tall, whole, whole, whole, wide, whole, tall, whole,
            ),
            check_vma=False,
        )(*args)

    return layer
```

```python
import functools
import math

import jax
import jax.numpy as jnp
from jax import lax
from jax.experimental import pallas as pl
from jax.experimental.pallas import tpu as pltpu
from jax.sharding import PartitionSpec as P

HD = 72
LEN = 1024
NORM_EPS = 1e-06
LOW = jnp.bfloat16
F32 = jnp.float32
SCALE = HD ** (-0.5)
SCALE_LOG2 = SCALE * math.log2(math.e)
VMEM_LIMIT = 50 * 1024 * 1024
GELU_A = math.sqrt(2 / math.pi)
GELU_B = 0.044715

NN = (((1,), (0,)), ((), ()))
NT = (((1,), (1,)), ((), ()))
TN = (((0,), (0,)), ((), ()))


def dot(left, right, dims=NN):
    return lax.dot_general(left, right, dims, preferred_element_type=F32)


def layer_norm(values, norm_gain, norm_shift):
    centred = values - jnp.mean(values, axis=-1, keepdims=True)
    spread = jnp.mean(centred * centred, axis=-1, keepdims=True)
    return centred * lax.rsqrt(spread + NORM_EPS) * norm_gain + norm_shift


def tie(value, *others):
    others = [other for other in others if other is not None]
    return lax.optimization_barrier((value, *others))[0] if others else value


def start_pieces(count, first, table_ref, sources, target_ref, sem):
    rows = target_ref.shape[0] // count

    def each(start):
        for n in range(count):
            slot = table_ref[n]
            for at, source in enumerate(sources):
                @pl.when((slot >= at * first) & (slot < (at + 1) * first))
                def _():
                    copy = pltpu.make_async_copy(
                        source.at[slot - at * first], target_ref.at[pl.ds(n * rows, rows)], sem.at[n]
                    )
                    if start:
                        copy.start()
                    else:
                        copy.wait()

    each(True)
    return functools.partial(each, False)


def attend_forward_body(heads, count, first, table_ref, rows_ref, bias_ref, *refs):
    sources, (qkv_ref, mixed_ref, lse_ref, weight_ref, sem) = refs[:-5], refs[-5:]
    wait = start_pieces(count, first, table_ref, sources, weight_ref, sem)
    wait()
    cols = heads * HD
    step = LEN // 2
    for part in range(2):
        at = pl.ds(part * step, step)
        qkv_ref[at, :] = (dot(rows_ref[at, :], weight_ref[...]) + bias_ref[...]).astype(LOW)
    for h in range(heads):
        lo = h * HD
        queries = qkv_ref[:, lo : lo + HD]
        keys = qkv_ref[:, cols + lo : cols + lo + HD]
        values = qkv_ref[:, 2 * cols + lo : 2 * cols + lo + HD]
        scores = dot(keys, queries, NT)
        highest = jnp.max(scores, axis=0, keepdims=True)
        probs = jnp.exp2((scores - highest) * SCALE_LOG2)
        total = jnp.sum(probs, axis=0, keepdims=True)
        mixed = dot(values.T, probs.astype(LOW)) / total
        lse_ref[h : h + 1, :] = highest * SCALE_LOG2 + jnp.log2(total)
        mixed_ref[:, lo : lo + HD] = mixed.T.astype(LOW)


def kernel_call(body, name, n_vmem, weight, out_shape, flops, transcendentals, scratch=()):
    sources, count = weight.sources, weight.count
    shape = sources[0].shape
    moved = sum(math.prod(o.shape) * o.dtype.itemsize for o in out_shape) + 2 * count * shape[1] * shape[2]
    return pl.pallas_call(
        functools.partial(body, count, shape[0]),
        in_specs=[pl.BlockSpec(memory_space=pltpu.SMEM)]
        + [pl.BlockSpec(memory_space=pltpu.VMEM)] * n_vmem
        + [pl.BlockSpec(memory_space=pl.ANY)] * len(sources),
        out_specs=[pl.BlockSpec(memory_space=pltpu.VMEM)] * len(out_shape),
        out_shape=out_shape,
        scratch_shapes=[*scratch, pltpu.SemaphoreType.DMA((count,))],
        compiler_params=pltpu.CompilerParams(vmem_limit_bytes=VMEM_LIMIT),
        cost_estimate=pl.CostEstimate(flops=flops, bytes_accessed=moved, transcendentals=transcendentals),
        name=name,
    )


class Weight:
    def __init__(self, sources, table):
        images, n_dp = table.shape
        _, rows, cols = sources[0].shape
        self.width = n_dp * rows
        if rows % 16:
            whole = jnp.take(jnp.concatenate(sources, axis=0), table.reshape(-1), axis=0)
            sources = (whole.reshape(images, self.width, cols),)
            table = jnp.arange(images, dtype=jnp.int32)[:, None]
        self.sources, self.table, self.count, self.cols = sources, table, table.shape[1], cols
        self.shape = jax.ShapeDtypeStruct((self.width, cols), LOW)


def attend_forward(rows, bias, weight, i, heads):
    cols = heads * HD
    return kernel_call(
        functools.partial(attend_forward_body, heads),
        "attend_forward",
        2,
        weight,
        [
            jax.ShapeDtypeStruct((LEN, 3 * cols), LOW),
            jax.ShapeDtypeStruct((LEN, cols), LOW),
            jax.ShapeDtypeStruct((heads, LEN), F32),
            weight.shape,
        ],
        heads * LEN * LEN * 1536 + 2 * LEN * weight.width * 3 * cols,
        heads * LEN * LEN,
    )(weight.table[i], rows, bias, *weight.sources)


def place_body(count, first, table_ref, *refs):
    sources, (weight_ref, sem) = refs[:-2], refs[-2:]
    start_pieces(count, first, table_ref, sources, weight_ref, sem)()


def placed(weight, i, name):
    return kernel_call(place_body, name, 0, weight, [weight.shape], 0, 0)(weight.table[i], *weight.sources)[0]


def up_body(count, first, table_ref, rows_ref, bias_ref, *refs):
    sources, (act_ref, slope_ref, weight_ref, sem) = refs[:-4], refs[-4:]
    start_pieces(count, first, table_ref, sources, weight_ref, sem)()
    step = LEN // 2
    for part in range(2):
        at = pl.ds(part * step, step)
        u = dot(rows_ref[at, :], weight_ref[...]) + bias_ref[...]
        square = u * u
        bend = jnp.tanh(u * (GELU_A + GELU_A * GELU_B * square))
        half = 0.5 + 0.5 * bend
        act_ref[at, :] = (u * half).astype(LOW)
        inner = u * (GELU_A + 3 * GELU_A * GELU_B * square)
        slope_ref[at, :] = (half + 0.5 * inner * (1 - bend * bend)).astype(LOW)


def up(rows, bias, weight, i):
    hidden = jax.ShapeDtypeStruct((LEN, weight.cols), LOW)
    return kernel_call(
        up_body, "up", 2, weight, [hidden, hidden, weight.shape],
        2 * LEN * weight.width * weight.cols, LEN * weight.cols,
    )(weight.table[i], rows, bias, *weight.sources)


def pre_grad_body(count, first, table_ref, rows_ref, slope_ref, *refs):
    sources, (grad_ref, bias_ref, weight_ref, sem) = refs[:-4], refs[-4:]
    start_pieces(count, first, table_ref, sources, weight_ref, sem)()
    step = LEN // 2
    for part in range(2):
        at = pl.ds(part * step, step)
        grad = (dot(rows_ref[at, :], weight_ref[...]) * slope_ref[at, :].astype(F32)).astype(LOW)
        grad_ref[at, :] = grad
        total = jnp.sum(grad.astype(F32), axis=0, keepdims=True)
        bias_ref[...] = total if part == 0 else bias_ref[...] + total


def pre_grad(rows, slope, weight, i):
    return kernel_call(
        pre_grad_body, "pre_grad", 2, weight,
        [jax.ShapeDtypeStruct((LEN, weight.cols), LOW), jax.ShapeDtypeStruct((1, weight.cols), F32), weight.shape],
        2 * LEN * weight.width * weight.cols, 0,
    )(weight.table[i], rows, slope, *weight.sources)


def attend_backward_body(heads, qkv_ref, grad_ref, mixed_ref, lse_ref, out_ref):
    cols = heads * HD
    for h in range(heads):
        lo = h * HD
        queries = qkv_ref[:, lo : lo + HD]
        keys = qkv_ref[:, cols + lo : cols + lo + HD]
        values = qkv_ref[:, 2 * cols + lo : 2 * cols + lo + HD]
        grads = grad_ref[:, lo : lo + HD]
        products = grads.astype(F32) * mixed_ref[:, lo : lo + HD].astype(F32)
        delta = jnp.sum(products.T, axis=0, keepdims=True)
        probs = jnp.exp2(dot(keys, queries, NT) * SCALE_LOG2 - lse_ref[h : h + 1, :])
        prob_grad = dot(values, grads, NT)
        out_ref[:, 2 * cols + lo : 2 * cols + lo + HD] = dot(probs.astype(LOW), grads).astype(LOW)
        score_grad = (probs * (prob_grad - delta)).astype(LOW)
        out_ref[:, cols + lo : cols + lo + HD] = (dot(score_grad, queries) * SCALE).astype(LOW)
        out_ref[:, lo : lo + HD] = (dot(keys.T, score_grad) * SCALE).T.astype(LOW)


def attend_backward(qkv, grads, mixed, lse, heads):
    rows, cols = grads.shape
    return pl.pallas_call(
        functools.partial(attend_backward_body, heads),
        in_specs=[pl.BlockSpec(memory_space=pltpu.VMEM)] * 4,
        out_specs=pl.BlockSpec(memory_space=pltpu.VMEM),
        out_shape=jax.ShapeDtypeStruct((rows, 3 * cols), LOW),
        compiler_params=pltpu.CompilerParams(vmem_limit_bytes=VMEM_LIMIT),
        cost_estimate=pl.CostEstimate(
            flops=heads * rows * rows * 4096,
            bytes_accessed=rows * cols * 18,
            transcendentals=heads * rows * rows,
        ),
        name="attend_backward",
    )(qkv, grads, mixed, lse)


def weight_grad_body(images, n_dp, half, table_ref, left_ref, *refs):
    rights, (keep_ref, send_ref, turned, product, sem) = refs[:images], refs[images:]
    width = turned.shape[0]
    shard_rows = width // n_dp
    turned[...] = left_ref[...].T
    step = width // 2

    def piece(start, n):
        slot = table_ref[n]
        source = product.at[n // n_dp, pl.ds((n % n_dp) * shard_rows, shard_rows)]
        for out_ref, mine, index in ((keep_ref, slot < half, slot), (send_ref, slot >= half, slot - half)):
            @pl.when(mine)
            def _():
                copy = pltpu.make_async_copy(source, out_ref.at[index], sem.at[n])
                if start:
                    copy.start()
                else:
                    copy.wait()

    for i in range(images):
        for part in range(2):
            at = pl.ds(part * step, step)
            product[i, at, :] = dot(turned[at, :], rights[i][...]).astype(LOW)
            for d in range(part * n_dp // 2, (part + 1) * n_dp // 2):
                piece(True, i * n_dp + d)
    for n in range(images * n_dp):
        piece(False, n)


def weight_grad(table, left, rights, n_dp, name):
    images = len(rights)
    rows, width = left.shape
    cols = rights[0].shape[1]
    shard_rows = width // n_dp
    half = images * n_dp // 2
    if shard_rows % 16:
        whole = jnp.concatenate([dot(left, right, TN).astype(LOW) for right in rights], axis=0)
        slots = whole.reshape(images * n_dp, shard_rows, cols)
        order = jnp.zeros_like(table).at[table].set(jnp.arange(table.shape[0], dtype=jnp.int32))
        slots = jnp.take(slots, order, axis=0)
        return slots[:half], slots[half:]
    shape = jax.ShapeDtypeStruct((half, shard_rows, cols), LOW)
    return pl.pallas_call(
        functools.partial(weight_grad_body, images, n_dp, half),
        in_specs=[pl.BlockSpec(memory_space=pltpu.SMEM)] + [pl.BlockSpec(memory_space=pltpu.VMEM)] * (1 + images),
        out_specs=[pl.BlockSpec(memory_space=pl.ANY)] * 2,
        out_shape=[shape, shape],
        scratch_shapes=[
            pltpu.VMEM((width, rows), LOW),
            pltpu.VMEM((images, width, cols), LOW),
            pltpu.SemaphoreType.DMA((images * n_dp,)),
        ],
        compiler_params=pltpu.CompilerParams(vmem_limit_bytes=VMEM_LIMIT),
        cost_estimate=pl.CostEstimate(
            flops=2 * images * rows * width * cols,
            bytes_accessed=2 * (rows * width + images * (rows + width) * cols),
            transcendentals=0,
        ),
        name=name,
    )(table, left, *rights)


class Plan:
    def __init__(self, n_dp, n_t, ranks):
        self.n_dp, self.n_t, self.ranks = n_dp, n_t, ranks
        self.images = n_t // ranks
        dims = [("dp", 1 << b) for b in reversed(range(n_dp.bit_length() - 1))]
        image_dims = [("image", 1 << b) for b in reversed(range(self.images.bit_length() - 1))]
        even = dims + image_dims
        odd = list(even)
        if image_dims and dims:
            odd[-2], odd[-1] = odd[-1], odd[-2]
        self.orders = (even, odd)
        self.stages = len(even)
        self.rank_stages = ranks.bit_length() - 1

    def permute(self, values, partner):
        pairs = []
        for d in range(self.n_dp):
            for t in range(self.n_t):
                d2, i2, r2 = partner(d, t // self.ranks, t % self.ranks)
                pairs.append((d * self.n_t + t, d2 * self.n_t + i2 * self.ranks + r2))
        return lax.ppermute(values, ("dp", "tensor"), pairs)

    def exchange(self, values, stage):
        def partner(d, i, r):
            kind, step = self.orders[r & 1][stage]
            return (d ^ step, i, r) if kind == "dp" else (d, i ^ step, r)

        return self.permute(values, partner)

    def rank_exchange(self, values, stage):
        return self.permute(values, lambda d, i, r: (d, i, r ^ (1 << stage)))

    def slots(self):
        me_dp, me_t = lax.axis_index("dp"), lax.axis_index("tensor")
        flips = jnp.arange(self.n_dp, dtype=jnp.int32)[None, :] ^ me_dp
        images = jnp.arange(self.images, dtype=jnp.int32)[:, None]

        def table(order):
            total = jnp.zeros((self.images, self.n_dp), jnp.int32)
            for stage, (kind, step) in enumerate(order):
                source = flips if kind == "dp" else images
                total = total + jnp.where((source & step) != 0, 1 << stage, 0)
            return total

        return jnp.where((me_t % self.ranks) & 1, table(self.orders[1]), table(self.orders[0]))

    def gather(self, shards):
        near = max(self.stages - 2, 0)
        held = [shard[None] for shard in shards]
        halves = [None] * len(shards)
        queues = ([], [])
        for n in range(len(shards)):
            for stage in range(self.stages):
                queue = queues[stage >= near]
                mine = tie(held[n], *queue[-2:-1])
                theirs = self.exchange(mine, stage)
                queue.append(theirs)
                if stage == self.stages - 1:
                    halves[n] = (mine, theirs)
                else:
                    held[n] = jnp.concatenate([mine, theirs], axis=0)
        return [Weight(half, self.slots()) for half in halves]

    def scatter(self, keep, send):
        for stage in reversed(range(self.stages)):
            theirs = self.exchange(send, stage)
            half = keep.shape[0] // 2
            if stage == 0:
                return (keep.astype(F32) + theirs.astype(F32))[0]
            send = (keep[half:].astype(F32) + theirs[half:].astype(F32)).astype(LOW)
            keep = (keep[:half].astype(F32) + theirs[:half].astype(F32)).astype(LOW)

    def total(self, values):
        for stage in range(self.rank_stages):
            values = values + self.rank_exchange(values, stage)
        for stage in range(self.stages):
            values = values + self.exchange(values, stage)
        return values

    def rank_gather(self, shard):
        mine = shard
        for stage in range(self.rank_stages):
            mine = jnp.concatenate([mine, self.rank_exchange(mine, stage)], axis=0)
        return mine

    def rank_scatter(self, rows):
        for stage in reversed(range(self.rank_stages)):
            half = rows.shape[0] // 2
            theirs = self.rank_exchange(rows[half:].astype(LOW), stage)
            rows = rows[:half] + theirs.astype(F32)
        return rows


def local(
    tokens, gain_one, shift_one, w_query, b_query, w_key, w_value, b_value, w_out, b_out,
    gain_two, shift_two, w_up, b_up, w_down, b_down, cotangent, plan=None,
):
    images, ranks, n_dp = plan.images, plan.ranks, plan.n_dp
    shard_rows = w_query.shape[0]
    width = tokens.shape[1]
    head_cols, hidden_cols = w_query.shape[1], w_up.shape[1]
    heads = head_cols // HD
    me_t = lax.axis_index("tensor")
    me_image, me_rank = me_t // ranks, me_t % ranks
    slot_table = plan.slots().reshape(-1)

    def shard_of(i):
        return (me_image ^ i) * ranks + me_rank

    def columns(vector, cols):
        return [lax.dynamic_slice_in_dim(vector, shard_of(i) * cols, cols) for i in range(images)]

    def uncolumns(parts, length):
        cols = parts[0].shape[0]
        blank = jnp.zeros((length,), F32)
        for i in range(images):
            blank = lax.dynamic_update_slice_in_dim(blank, parts[i], shard_of(i) * cols, 0)
        return blank

    def scattered(left, rights, name):
        return plan.scatter(*weight_grad(slot_table, left, rights, n_dp, name))

    def low(values):
        return values.astype(LOW)

    each = range(images)
    weights = plan.gather(
        [
            jnp.concatenate([low(w_query), low(w_key), low(w_value)], axis=1),
            low(w_out).T,
            low(w_up),
            low(w_down).T,
        ]
    )
    qkv_weight, out_weight, up_weight, down_weight = weights

    cot_rows = plan.rank_gather(cotangent)
    inputs32 = tokens.astype(F32)
    normed_one = low(layer_norm(inputs32, gain_one, shift_one))
    rows_one = plan.rank_gather(normed_one)
    query_bias, value_bias = columns(b_query, head_cols), columns(b_value, head_cols)
    blank = jnp.zeros((head_cols,), F32)
    qkv, mixed, lse, qkv_full = zip(
        *(
            attend_forward(
                rows_one, jnp.concatenate([query_bias[i], blank, value_bias[i]])[None], qkv_weight, i, heads
            )
            for i in each
        )
    )

    out_full = [placed(out_weight, i, "place_out") for i in each]
    attn = sum(dot(mixed[i], out_full[i], NT) for i in each)
    residual = inputs32 + plan.rank_scatter(attn) + b_out
    normed_two = low(layer_norm(residual, gain_two, shift_two))
    rows_two = plan.rank_gather(normed_two)
    up_bias = columns(b_up, hidden_cols)
    act, slope, up_full = zip(*(up(rows_two, up_bias[i][None], up_weight, i) for i in each))
    down_grad = scattered(cot_rows, act, "grad_down").T

    grad_out = cotangent.astype(F32)
    down_bias_grad = jnp.sum(grad_out, axis=0)
    pre_low, up_bias_parts, down_full = zip(*(pre_grad(cot_rows, slope[i], down_weight, i) for i in each))
    up_grad = scattered(rows_two, pre_low, "grad_up")
    up_bias_grad = uncolumns([part[0] for part in up_bias_parts], b_up.shape[0])
    norm_two_grad = plan.rank_scatter(sum(dot(pre_low[i], up_full[i], NT) for i in each))
    _, pull_two = jax.vjp(layer_norm, residual, gain_two, shift_two)
    residual_part, gain_two_grad, shift_two_grad = pull_two(norm_two_grad)
    residual_grad = grad_out + residual_part
    branch_low = low(residual_grad)
    out_bias_grad = jnp.sum(branch_low, axis=0, dtype=F32)
    branch_rows = plan.rank_gather(branch_low)

    mlp = sum(dot(act[i], down_full[i], NT) for i in each)
    output = low(residual + plan.rank_scatter(mlp) + b_down)

    mixed_grad = [low(dot(branch_rows, out_full[i])) for i in each]
    out_grad = scattered(branch_rows, mixed, "grad_out").T
    qkv_grads = [attend_backward(qkv[i], mixed_grad[i], mixed[i], lse[i], heads) for i in each]
    qkv_grad = scattered(rows_one, qkv_grads, "grad_qkv")
    query_grad, key_grad, value_grad = (qkv_grad[:, n * head_cols : (n + 1) * head_cols] for n in range(3))
    qkv_sums = [jnp.sum(grads, axis=0, dtype=F32) for grads in qkv_grads]
    query_bias_grad = uncolumns([sums[:head_cols] for sums in qkv_sums], b_query.shape[0])
    value_bias_grad = uncolumns([sums[2 * head_cols :] for sums in qkv_sums], b_value.shape[0])
    norm_one_grad = plan.rank_scatter(sum(dot(qkv_grads[i], qkv_full[i], NT) for i in each))
    _, pull_one = jax.vjp(layer_norm, inputs32, gain_one, shift_one)
    input_part, gain_one_grad, shift_one_grad = pull_one(norm_one_grad)
    grad_tokens = low(residual_grad + input_part)

    vectors = [
        gain_one_grad, shift_one_grad, query_bias_grad, value_bias_grad, out_bias_grad,
        gain_two_grad, shift_two_grad, up_bias_grad, down_bias_grad,
    ]
    lengths = [vector.shape[0] for vector in vectors]
    together = plan.total(jnp.concatenate([*vectors, jnp.zeros((-sum(lengths) % 1024,), F32)]))
    small, begin = [], 0
    for length in lengths:
        small.append(together[begin : begin + length])
        begin += length
    return (
        output, grad_tokens, small[0], small[1], query_grad, small[2], key_grad, value_grad, small[3],
        out_grad, small[4], small[5], small[6], up_grad, small[7], down_grad, small[8],
    )


def solution(mesh):
    split = P(("dp", "tensor"), None)
    whole, wide, tall = P(), P("dp", "tensor"), P("tensor", "dp")
    n_dp, n_t = mesh.shape["dp"], mesh.shape["tensor"]

    def layer(*args):
        rows = args[0].shape[0] // (n_dp * n_t)
        plan = Plan(n_dp, n_t, LEN // rows)
        return jax.shard_map(
            functools.partial(local, plan=plan),
            mesh=mesh,
            in_specs=(
                split, whole, whole, wide, whole, wide, wide, whole, tall, whole,
                whole, whole, wide, whole, tall, whole, split,
            ),
            out_specs=(
                split, split, whole, whole, wide, whole, wide, wide, whole,
                tall, whole, whole, whole, wide, whole, tall, whole,
            ),
            check_vma=False,
        )(*args)

    return layer
```

```python
import functools
import math

import jax
import jax.numpy as jnp
from jax import lax
from jax.experimental import pallas as pl
from jax.experimental.pallas import tpu as pltpu
from jax.sharding import PartitionSpec as P

HD = 72
LEN = 1024
NORM_EPS = 1e-06
LOW = jnp.bfloat16
F32 = jnp.float32
SCALE = HD ** (-0.5)
SCALE_LOG2 = SCALE * math.log2(math.e)
VMEM_LIMIT = 50 * 1024 * 1024
GELU_A = math.sqrt(2 / math.pi)
GELU_B = 0.044715
SHORT = pl.CostEstimate(flops=0, bytes_accessed=0, transcendentals=0)

NN = (((1,), (0,)), ((), ()))
NT = (((1,), (1,)), ((), ()))
TN = (((0,), (0,)), ((), ()))


def dot(left, right, dims=NN):
    return lax.dot_general(left, right, dims, preferred_element_type=F32)


def layer_norm(values, norm_gain, norm_shift):
    centred = values - jnp.mean(values, axis=-1, keepdims=True)
    spread = jnp.mean(centred * centred, axis=-1, keepdims=True)
    return centred * lax.rsqrt(spread + NORM_EPS) * norm_gain + norm_shift


def tie(values, others):
    if not others:
        return values
    return lax.optimization_barrier((*values, *others))[: len(values)]


class Order:
    def __init__(self):
        self.done, self.begun = [], []

    def enter(self, operand):
        return tie((operand,), [*self.done, *self.begun])[0]

    def leave(self, result):
        self.done, self.begun = [result], []


def start_pieces(count, first, table_ref, sources, target_ref, sem):
    rows = target_ref.shape[0] // count

    def each(start):
        for n in range(count):
            slot = table_ref[n]
            for at, source in enumerate(sources):
                @pl.when((slot >= at * first) & (slot < (at + 1) * first))
                def _():
                    copy = pltpu.make_async_copy(
                        source.at[slot - at * first], target_ref.at[pl.ds(n * rows, rows)], sem.at[n]
                    )
                    if start:
                        copy.start()
                    else:
                        copy.wait()

    each(True)
    return functools.partial(each, False)


def spans(parts):
    begin = 0
    for part in parts:
        yield part, pl.ds(begin, part.shape[0])
        begin += part.shape[0]


def attend_forward_body(heads, n_parts, count, first, table_ref, bias_ref, *refs):
    parts, sources, (qkv_ref, mixed_ref, lse_ref, weight_ref, sem) = refs[:n_parts], refs[n_parts:-5], refs[-5:]
    start_pieces(count, first, table_ref, sources, weight_ref, sem)()
    cols = heads * HD
    for part, at in spans(parts):
        qkv_ref[at, :] = (dot(part[...], weight_ref[...]) + bias_ref[...]).astype(LOW)
    for h in range(heads):
        lo = h * HD
        queries = qkv_ref[:, lo : lo + HD]
        keys = qkv_ref[:, cols + lo : cols + lo + HD]
        values = qkv_ref[:, 2 * cols + lo : 2 * cols + lo + HD]
        scores = dot(keys, queries, NT)
        highest = jnp.max(scores, axis=0, keepdims=True)
        probs = jnp.exp2((scores - highest) * SCALE_LOG2)
        total = jnp.sum(probs, axis=0, keepdims=True)
        mixed = dot(values.T, probs.astype(LOW)) / total
        lse_ref[h : h + 1, :] = highest * SCALE_LOG2 + jnp.log2(total)
        mixed_ref[:, lo : lo + HD] = mixed.T.astype(LOW)


def kernel_call(body, name, n_vmem, weight, out_shape, flops, transcendentals, scratch=()):
    sources, count = weight.sources, weight.count
    shape = sources[0].shape
    moved = sum(math.prod(o.shape) * o.dtype.itemsize for o in out_shape) + 2 * count * shape[1] * shape[2]
    return pl.pallas_call(
        functools.partial(body, count, shape[0]),
        in_specs=[pl.BlockSpec(memory_space=pltpu.SMEM)]
        + [pl.BlockSpec(memory_space=pltpu.VMEM)] * n_vmem
        + [pl.BlockSpec(memory_space=pl.ANY)] * len(sources),
        out_specs=[pl.BlockSpec(memory_space=pltpu.VMEM)] * len(out_shape),
        out_shape=out_shape,
        scratch_shapes=[*scratch, pltpu.SemaphoreType.DMA((count,))],
        compiler_params=pltpu.CompilerParams(vmem_limit_bytes=VMEM_LIMIT),
        cost_estimate=SHORT,
        name=name,
    )


class Weight:
    def __init__(self, sources, table):
        images, n_dp = table.shape
        _, rows, cols = sources[0].shape
        self.width = n_dp * rows
        if rows % 16:
            whole = jnp.take(jnp.concatenate(sources, axis=0), table.reshape(-1), axis=0)
            sources = (whole.reshape(images, self.width, cols),)
            table = jnp.arange(images, dtype=jnp.int32)[:, None]
        self.sources, self.table, self.count, self.cols = sources, table, table.shape[1], cols
        self.shape = jax.ShapeDtypeStruct((self.width, cols), LOW)


def attend_forward(bias, parts, weight, i, heads):
    cols = heads * HD
    return kernel_call(
        functools.partial(attend_forward_body, heads, len(parts)),
        "attend_forward",
        1 + len(parts),
        weight,
        [
            jax.ShapeDtypeStruct((LEN, 3 * cols), LOW),
            jax.ShapeDtypeStruct((LEN, cols), LOW),
            jax.ShapeDtypeStruct((heads, LEN), F32),
            weight.shape,
        ],
        heads * LEN * LEN * 1536 + 2 * LEN * weight.width * 3 * cols,
        heads * LEN * LEN,
    )(weight.table[i], bias, *parts, *weight.sources)


def place_body(count, first, table_ref, *refs):
    sources, (weight_ref, sem) = refs[:-2], refs[-2:]
    start_pieces(count, first, table_ref, sources, weight_ref, sem)()


def placed(weight, enter, i, name):
    return kernel_call(place_body, name, 0, weight, [weight.shape], 0, 0)(enter(weight.table[i]), *weight.sources)[0]


def up_body(n_parts, count, first, table_ref, bias_ref, *refs):
    parts, sources, (act_ref, slope_ref, weight_ref, sem) = refs[:n_parts], refs[n_parts:-4], refs[-4:]
    start_pieces(count, first, table_ref, sources, weight_ref, sem)()
    for part, at in spans(parts):
        u = dot(part[...], weight_ref[...]) + bias_ref[...]
        square = u * u
        bend = jnp.tanh(u * (GELU_A + GELU_A * GELU_B * square))
        half = 0.5 + 0.5 * bend
        act_ref[at, :] = (u * half).astype(LOW)
        inner = u * (GELU_A + 3 * GELU_A * GELU_B * square)
        slope_ref[at, :] = (half + 0.5 * inner * (1 - bend * bend)).astype(LOW)


def up(bias, parts, weight, i):
    hidden = jax.ShapeDtypeStruct((LEN, weight.cols), LOW)
    return kernel_call(
        functools.partial(up_body, len(parts)), "up", 1 + len(parts), weight, [hidden, hidden, weight.shape],
        2 * LEN * weight.width * weight.cols, LEN * weight.cols,
    )(weight.table[i], bias, *parts, *weight.sources)


def pre_grad_body(n_parts, count, first, table_ref, slope_ref, *refs):
    parts, sources, (grad_ref, bias_ref, weight_ref, sem) = refs[:n_parts], refs[n_parts:-4], refs[-4:]
    start_pieces(count, first, table_ref, sources, weight_ref, sem)()
    bias_ref[...] = jnp.zeros_like(bias_ref)
    for part, at in spans(parts):
        grad = (dot(part[...], weight_ref[...]) * slope_ref[at, :].astype(F32)).astype(LOW)
        grad_ref[at, :] = grad
        bias_ref[...] += jnp.sum(grad.astype(F32), axis=0, keepdims=True)


def pre_grad(table, slope, parts, weight):
    return kernel_call(
        functools.partial(pre_grad_body, len(parts)), "pre_grad", 1 + len(parts), weight,
        [jax.ShapeDtypeStruct((LEN, weight.cols), LOW), jax.ShapeDtypeStruct((1, weight.cols), F32), weight.shape],
        2 * LEN * weight.width * weight.cols, 0,
    )(table, slope, *parts, *weight.sources)


def attend_backward_body(heads, lse_ref, qkv_ref, mixed_ref, out_ref, *refs):
    parts, (grads_ref, grad_ref) = refs[:-2], refs[-2:]
    cols = heads * HD
    for part, at in spans(parts):
        grad_ref[at, :] = dot(part[...], out_ref[...]).astype(LOW)
    for h in range(heads):
        lo = h * HD
        queries = qkv_ref[:, lo : lo + HD]
        keys = qkv_ref[:, cols + lo : cols + lo + HD]
        values = qkv_ref[:, 2 * cols + lo : 2 * cols + lo + HD]
        grads = grad_ref[:, lo : lo + HD]
        products = grads.astype(F32) * mixed_ref[:, lo : lo + HD].astype(F32)
        delta = jnp.sum(products.T, axis=0, keepdims=True)
        probs = jnp.exp2(dot(keys, queries, NT) * SCALE_LOG2 - lse_ref[h : h + 1, :])
        prob_grad = dot(values, grads, NT)
        grads_ref[:, 2 * cols + lo : 2 * cols + lo + HD] = dot(probs.astype(LOW), grads).astype(LOW)
        score_grad = (probs * (prob_grad - delta)).astype(LOW)
        grads_ref[:, cols + lo : cols + lo + HD] = (dot(score_grad, queries) * SCALE).astype(LOW)
        grads_ref[:, lo : lo + HD] = (dot(keys.T, score_grad) * SCALE).T.astype(LOW)


def attend_backward(lse, qkv, mixed, out_full, parts, heads):
    rows, cols = mixed.shape
    return pl.pallas_call(
        functools.partial(attend_backward_body, heads),
        in_specs=[pl.BlockSpec(memory_space=pltpu.VMEM)] * (4 + len(parts)),
        out_specs=pl.BlockSpec(memory_space=pltpu.VMEM),
        out_shape=jax.ShapeDtypeStruct((rows, 3 * cols), LOW),
        scratch_shapes=[pltpu.VMEM((rows, cols), LOW)],
        compiler_params=pltpu.CompilerParams(vmem_limit_bytes=VMEM_LIMIT),
        cost_estimate=SHORT,
        name="attend_backward",
    )(lse, qkv, mixed, out_full, *parts)


def weight_grad_body(images, n_dp, half, table_ref, *refs):
    lefts, rights, (keep_ref, send_ref, turned, product, sem) = refs[: -5 - images], refs[-5 - images : -5], refs[-5:]
    width = turned.shape[0]
    shard_rows = width // n_dp
    for left, at in spans(lefts):
        turned[:, at] = left[...].T
    step = width // 2

    def piece(start, n):
        slot = table_ref[n]
        source = product.at[n // n_dp, pl.ds((n % n_dp) * shard_rows, shard_rows)]
        for out_ref, mine, index in ((keep_ref, slot < half, slot), (send_ref, slot >= half, slot - half)):
            @pl.when(mine)
            def _():
                copy = pltpu.make_async_copy(source, out_ref.at[index], sem.at[n])
                if start:
                    copy.start()
                else:
                    copy.wait()

    for i in range(images):
        for part in range(2):
            at = pl.ds(part * step, step)
            product[i, at, :] = dot(turned[at, :], rights[i][...]).astype(LOW)
            for d in range(part * n_dp // 2, (part + 1) * n_dp // 2):
                piece(True, i * n_dp + d)
    for n in range(images * n_dp):
        piece(False, n)


def weight_grad(table, lefts, rights, n_dp, name):
    images = len(rights)
    rows, width = LEN, lefts[0].shape[1]
    cols = rights[0].shape[1]
    shard_rows = width // n_dp
    half = images * n_dp // 2
    if shard_rows % 16:
        left = jnp.concatenate(lefts, axis=0)
        whole = jnp.concatenate([dot(left, right, TN).astype(LOW) for right in rights], axis=0)
        slots = whole.reshape(images * n_dp, shard_rows, cols)
        order = jnp.zeros_like(table).at[table].set(jnp.arange(table.shape[0], dtype=jnp.int32))
        slots = jnp.take(slots, order, axis=0)
        return slots[:half], slots[half:]
    shape = jax.ShapeDtypeStruct((half, shard_rows, cols), LOW)
    return pl.pallas_call(
        functools.partial(weight_grad_body, images, n_dp, half),
        in_specs=[pl.BlockSpec(memory_space=pltpu.SMEM)] + [pl.BlockSpec(memory_space=pltpu.VMEM)] * (len(lefts) + images),
        out_specs=[pl.BlockSpec(memory_space=pl.ANY)] * 2,
        out_shape=[shape, shape],
        scratch_shapes=[
            pltpu.VMEM((width, rows), LOW),
            pltpu.VMEM((images, width, cols), LOW),
            pltpu.SemaphoreType.DMA((images * n_dp,)),
        ],
        compiler_params=pltpu.CompilerParams(vmem_limit_bytes=VMEM_LIMIT),
        cost_estimate=SHORT,
        name=name,
    )(table, *lefts, *rights)


class Plan:
    def __init__(self, n_dp, n_t, ranks):
        self.n_dp, self.n_t, self.ranks = n_dp, n_t, ranks
        self.images = n_t // ranks
        dims = [("dp", 1 << b) for b in reversed(range(n_dp.bit_length() - 1))]
        image_dims = [("image", 1 << b) for b in reversed(range(self.images.bit_length() - 1))]
        even = dims + image_dims
        odd = list(even)
        if image_dims and dims:
            odd[-2], odd[-1] = odd[-1], odd[-2]
        self.orders = {"far": (even, odd), "near": tuple(way[-2:-1] + way[:-2] + way[-1:] for way in (even, odd))}
        self.stages = len(even)
        self.rank_stages = ranks.bit_length() - 1

    def permute(self, values, partner):
        pairs = []
        for d in range(self.n_dp):
            for t in range(self.n_t):
                d2, i2, r2 = partner(d, t // self.ranks, t % self.ranks)
                pairs.append((d * self.n_t + t, d2 * self.n_t + i2 * self.ranks + r2))
        return lax.ppermute(values, ("dp", "tensor"), pairs)

    def exchange(self, values, stage, way="far"):
        def partner(d, i, r):
            kind, step = self.orders[way][r & 1][stage]
            return (d ^ step, i, r) if kind == "dp" else (d, i ^ step, r)

        return self.permute(values, partner)

    def rank_exchange(self, values, stage):
        return self.permute(values, lambda d, i, r: (d, i, r ^ (1 << stage)))

    def slots(self, way="far"):
        me_dp, me_t = lax.axis_index("dp"), lax.axis_index("tensor")
        flips = jnp.arange(self.n_dp, dtype=jnp.int32)[None, :] ^ me_dp
        images = jnp.arange(self.images, dtype=jnp.int32)[:, None]

        def table(order):
            total = jnp.zeros((self.images, self.n_dp), jnp.int32)
            for stage, (kind, step) in enumerate(order):
                source = flips if kind == "dp" else images
                total = total + jnp.where((source & step) != 0, 1 << stage, 0)
            return total

        even, odd = self.orders[way]
        return jnp.where((me_t % self.ranks) & 1, table(odd), table(even))

    def rank_gather(self, shard):
        parts = [shard]
        for stage in range(self.rank_stages):
            mine = jnp.concatenate(parts, axis=0) if stage else shard
            parts.append(self.rank_exchange(mine, stage))
        return parts

    def rank_scatter(self, rows, *after):
        for stage in reversed(range(self.rank_stages)):
            half = rows.shape[0] // 2
            (theirs,) = tie((self.rank_exchange(rows[half:].astype(LOW), stage),), after)
            rows = rows[:half] + theirs.astype(F32)
        return rows


class Gather:
    def __init__(self, plan, order, shard, way="far"):
        self.plan, self.order, self.held, self.stage, self.way = plan, order, (shard[None],), 0, way

    def to(self, stage, *after):
        while self.stage < stage:
            held = tie(self.held, [*self.order.done, *after])
            mine = held[0] if len(held) == 1 else jnp.concatenate(held, axis=0)
            self.held = (mine, self.plan.exchange(mine, self.stage, self.way))
            self.order.begun.append(mine)
            self.stage += 1
        return self.held[-1]

    def weight(self):
        self.to(self.plan.stages)
        return Weight(self.held, self.plan.slots(self.way))


class Scatter:
    def __init__(self, plan, order, keep, send, way):
        self.plan, self.order, self.keep, self.send, self.way = plan, order, keep, send, way
        self.theirs, self.stage = None, plan.stages

    def total(self, part):
        return self.keep[part].astype(F32) + self.theirs[part].astype(F32)

    def to(self, stage, *after):
        while self.stage > stage:
            if self.theirs is not None:
                self.keep, self.theirs = tie((self.keep, self.theirs), [*self.order.done, *after])
                half = self.keep.shape[0] // 2
                self.send, self.keep = self.total(slice(half, None)).astype(LOW), self.total(slice(half)).astype(LOW)
            self.stage -= 1
            self.theirs = self.plan.exchange(self.send, self.stage, self.way)
            self.order.begun.append(self.send)
        return self.theirs

    def finish(self):
        self.to(0)
        return self.total(0)


def local(
    tokens, gain_one, shift_one, w_query, b_query, w_key, w_value, b_value, w_out, b_out,
    gain_two, shift_two, w_up, b_up, w_down, b_down, cotangent, plan=None,
):
    images, ranks, n_dp = plan.images, plan.ranks, plan.n_dp
    shard_rows = w_query.shape[0]
    width = tokens.shape[1]
    head_cols, hidden_cols = w_query.shape[1], w_up.shape[1]
    heads = head_cols // HD
    me_t = lax.axis_index("tensor")
    me_image, me_rank = me_t // ranks, me_t % ranks

    def shard_of(i):
        return (me_image ^ i) * ranks + me_rank

    def columns(vector, cols):
        return [lax.dynamic_slice_in_dim(vector, shard_of(i) * cols, cols) for i in range(images)]

    def uncolumns(parts, length):
        cols = parts[0].shape[0]
        blank = jnp.zeros((length,), F32)
        for i in range(images):
            blank = lax.dynamic_update_slice_in_dim(blank, parts[i], shard_of(i) * cols, 0)
        return blank

    order = Order()

    def scatter(lefts, rights, name, way="far"):
        table = plan.slots(way).reshape(-1)
        keep, send = weight_grad(order.enter(table), lefts, rights, n_dp, name)
        order.leave(send)
        begun = Scatter(plan, order, keep, send, way)
        begun.to(plan.stages - 1)
        return begun

    def low(values):
        return values.astype(LOW)

    each = range(images)
    last, near = plan.stages, max(plan.stages - 1, 0)
    far = max(plan.stages - 2, 0)
    first = max(plan.stages - 3, 0)
    gather_qkv = Gather(plan, order, jnp.concatenate([low(w_query), low(w_key), low(w_value)], axis=1))
    gather_out = Gather(plan, order, low(w_out).T)
    gather_up = Gather(plan, order, low(w_up))
    gather_down = Gather(plan, order, low(w_down).T, "near")
    cot_rows = plan.rank_gather(cotangent)
    inputs32 = tokens.astype(F32)
    normed_one = low(layer_norm(inputs32, gain_one, shift_one))
    rows_one = plan.rank_gather(normed_one)
    token = gather_qkv.to(first)
    down_token = gather_down.to(min(1, far))
    gather_qkv.to(far)
    out_token = gather_out.to(first, token)
    token = gather_qkv.held[-1]
    gather_qkv.to(near, out_token, down_token, rows_one[-1], cot_rows[-1])
    up_token = gather_up.to(first, token)
    out_token = gather_out.to(far, token)
    token = gather_qkv.held[-1]
    gather_qkv.to(last, out_token, up_token)
    gather_up.to(far, token)
    gather_out.to(near, gather_qkv.held[-1])
    gather_up.to(near, gather_qkv.held[-1])
    gather_down.to(near - 1, gather_up.held[0])
    order.begun = [gather_up.held[0], gather_down.held[0]]

    query_bias, value_bias = columns(b_query, head_cols), columns(b_value, head_cols)
    blank = jnp.zeros((head_cols,), F32)
    qkv, mixed, lse, qkv_full = [None] * images, [None] * images, [None] * images, [None] * images
    for i in each:
        bias = order.enter(jnp.concatenate([query_bias[i], blank, value_bias[i]])[None])
        qkv[i], mixed[i], lse[i], qkv_full[i] = attend_forward(bias, rows_one, gather_qkv.weight(), i, heads)
        order.leave(lse[i])
        if i == 0:
            gather_out.to(last)
            gather_up.to(last)
    gather_down.to(near)

    out_full = [placed(gather_out.weight(), order.enter, i, "place_out") for i in each]
    attn = sum(dot(mixed[i], out_full[i], NT) for i in each)
    residual = inputs32 + plan.rank_scatter(attn, gather_up.held[-1]) + b_out
    normed_two = low(layer_norm(residual, gain_two, shift_two))
    order.leave(normed_two[:8])
    rows_two = plan.rank_gather(normed_two)
    up_bias = columns(b_up, hidden_cols)
    act, slope, up_full = [None] * images, [None] * images, [None] * images
    for i in each:
        bias = order.enter(up_bias[i][None])
        act[i], slope[i], up_full[i] = up(bias, rows_two, gather_up.weight(), i)
        order.leave(act[i])
        if i == 0:
            gather_down.to(last)
    scatter_down = scatter(cot_rows, act, "grad_down", "near")

    grad_out = cotangent.astype(F32)
    down_bias_grad = jnp.sum(grad_out, axis=0)
    pre_low, up_bias_parts, down_full = [None] * images, [None] * images, [None] * images
    down_weight = gather_down.weight()
    for i in each:
        table = order.enter(down_weight.table[i])
        pre_low[i], up_bias_parts[i], down_full[i] = pre_grad(table, slope[i], cot_rows, down_weight)
        order.leave(up_bias_parts[i])
    partial_two = sum(dot(pre_low[i], up_full[i], NT) for i in each)
    order.leave(partial_two[:8])
    scatter_down.to(far)
    scatter_up = scatter(rows_two, pre_low, "grad_up")
    norm_two_grad = plan.rank_scatter(partial_two)
    up_bias_grad = uncolumns([part[0] for part in up_bias_parts], b_up.shape[0])
    _, pull_two = jax.vjp(layer_norm, residual, gain_two, shift_two)
    residual_part, gain_two_grad, shift_two_grad = pull_two(norm_two_grad)
    residual_grad = grad_out + residual_part
    branch_low = low(residual_grad)
    out_bias_grad = jnp.sum(branch_low, axis=0, dtype=F32)
    branch_rows = plan.rank_gather(branch_low)
    scatter_out = scatter(branch_rows, mixed, "grad_out")
    scatter_down.to(first)

    qkv_grads = []
    for i in each:
        start = order.enter(lse[i])
        qkv_grads.append(attend_backward(start, qkv[i], mixed[i], out_full[i], branch_rows, heads))
        order.leave(qkv_grads[i])
        if i == 0:
            scatter_up.to(far)
            scatter_out.to(far)
    scatter_qkv = scatter(rows_one, qkv_grads, "grad_qkv")
    scatter_up.to(first)
    scatter_out.to(first)
    scatter_down.to(0)
    partial_one = sum(dot(order.enter(qkv_grads[i]), qkv_full[i], NT) for i in each)
    order.leave(partial_one[:8])
    mlp = sum(dot(order.enter(act[i]), down_full[i], NT) for i in each)
    order.leave(mlp[:8])
    scatter_up.to(0)
    scatter_out.to(0)
    norm_one_grad = order.enter(plan.rank_scatter(partial_one))
    _, pull_one = jax.vjp(layer_norm, inputs32, gain_one, shift_one)
    input_part, gain_one_grad, shift_one_grad = pull_one(norm_one_grad)
    grad_tokens = low(residual_grad + input_part)
    output = low(residual + plan.rank_scatter(mlp) + b_down)
    order.leave(gain_one_grad)
    scatter_qkv.to(far)
    gain_one_grad = order.enter(gain_one_grad)
    down_grad = scatter_down.finish().T
    up_grad = scatter_up.finish()
    out_grad = scatter_out.finish().T
    qkv_sums = [jnp.sum(grads, axis=0, dtype=F32) for grads in qkv_grads]
    query_bias_grad = uncolumns([sums[:head_cols] for sums in qkv_sums], b_query.shape[0])
    value_bias_grad = uncolumns([sums[2 * head_cols :] for sums in qkv_sums], b_value.shape[0])

    vectors = [
        gain_one_grad, shift_one_grad, query_bias_grad, value_bias_grad, out_bias_grad,
        gain_two_grad, shift_two_grad, up_bias_grad, down_bias_grad,
    ]
    lengths = [vector.shape[0] for vector in vectors]
    together = jnp.concatenate([*vectors, jnp.zeros((-sum(lengths) % 1024,), F32)])
    for stage in range(plan.rank_stages):
        together = together + plan.rank_exchange(together, stage)
    for stage in range(plan.stages):
        together = together + plan.exchange(together, stage)
        if stage in (first, near):
            order.leave(together)
            if stage == first:
                scatter_qkv.to(first, up_grad, out_grad)
            else:
                scatter_qkv.to(0)
            together = order.enter(together)
    qkv_grad = scatter_qkv.finish()
    query_grad, key_grad, value_grad = (qkv_grad[:, n * head_cols : (n + 1) * head_cols] for n in range(3))
    small, begin = [], 0
    for length in lengths:
        small.append(together[begin : begin + length])
        begin += length
    return (
        output, grad_tokens, small[0], small[1], query_grad, small[2], key_grad, value_grad, small[3],
        out_grad, small[4], small[5], small[6], up_grad, small[7], down_grad, small[8],
    )


def solution(mesh):
    split = P(("dp", "tensor"), None)
    whole, wide, tall = P(), P("dp", "tensor"), P("tensor", "dp")
    n_dp, n_t = mesh.shape["dp"], mesh.shape["tensor"]

    def layer(*args):
        rows = args[0].shape[0] // (n_dp * n_t)
        plan = Plan(n_dp, n_t, LEN // rows)
        return jax.shard_map(
            functools.partial(local, plan=plan),
            mesh=mesh,
            in_specs=(
                split, whole, whole, wide, whole, wide, wide, whole, tall, whole,
                whole, whole, wide, whole, tall, whole, split,
            ),
            out_specs=(
                split, split, whole, whole, wide, whole, wide, wide, whole,
                tall, whole, whole, whole, wide, whole, tall, whole,
            ),
            check_vma=False,
        )(*args)

    return layer
```

```python
import functools
import math

import jax
import jax.numpy as jnp
from jax import lax
from jax.experimental import pallas as pl
from jax.experimental.pallas import tpu as pltpu
from jax.sharding import PartitionSpec as P

HD = 72
LEN = 1024
NORM_EPS = 1e-06
LOW = jnp.bfloat16
F32 = jnp.float32
SCALE = HD ** (-0.5)
SCALE_LOG2 = SCALE * math.log2(math.e)
VMEM_LIMIT = 50 * 1024 * 1024
GELU_A = math.sqrt(2 / math.pi)
GELU_B = 0.044715
SHORT = pl.CostEstimate(flops=0, bytes_accessed=0, transcendentals=0)

NN = (((1,), (0,)), ((), ()))
NT = (((1,), (1,)), ((), ()))
TN = (((0,), (0,)), ((), ()))


def dot(left, right, dims=NN):
    return lax.dot_general(left, right, dims, preferred_element_type=F32)


def layer_norm(values, norm_gain, norm_shift):
    centred = values - jnp.mean(values, axis=-1, keepdims=True)
    spread = jnp.mean(centred * centred, axis=-1, keepdims=True)
    return centred * lax.rsqrt(spread + NORM_EPS) * norm_gain + norm_shift


def tie(values, others):
    if not others:
        return values
    return lax.optimization_barrier((*values, *others))[: len(values)]


class Order:
    def __init__(self):
        self.done, self.begun = [], []

    def enter(self, operand):
        return tie((operand,), [*self.done, *self.begun])[0]

    def leave(self, result):
        self.done, self.begun = [result], []


def start_pieces(count, first, table_ref, sources, target_ref, sem):
    rows = target_ref.shape[0] // count

    def each(start):
        for n in range(count):
            slot = table_ref[n]
            for at, source in enumerate(sources):
                @pl.when((slot >= at * first) & (slot < (at + 1) * first))
                def _():
                    copy = pltpu.make_async_copy(
                        source.at[slot - at * first], target_ref.at[pl.ds(n * rows, rows)], sem.at[n]
                    )
                    if start:
                        copy.start()
                    else:
                        copy.wait()

    each(True)
    return functools.partial(each, False)


def spans(parts):
    begin = 0
    for part in parts:
        yield part, pl.ds(begin, part.shape[0])
        begin += part.shape[0]


def moves(pairs, sem, first=0):
    copies = [pltpu.make_async_copy(source, to, sem.at[first + n]) for n, (source, to) in enumerate(pairs)]
    for copy in copies:
        copy.start()
    return [copy.wait for copy in copies]


def load_parts(parts, rows_ref, sem):
    places = [at for _, at in spans(parts)]
    return list(zip(places, moves([(part, rows_ref.at[at]) for part, at in zip(parts, places)], sem)))


def attend_forward_body(heads, n_parts, count, first, table_ref, bias_ref, *refs):
    parts, sources = refs[:n_parts], refs[n_parts:-9]
    qkv_out, mixed_ref, lse_ref, weight_out, qkv_ref, weight_ref, rows_ref, sem, move_sem = refs[-9:]
    wait_pieces = start_pieces(count, first, table_ref, sources, weight_ref, sem)
    loads = load_parts(parts, rows_ref, move_sem)
    cols = heads * HD
    wait_pieces()
    outs = moves([(weight_ref, weight_out)], move_sem, n_parts)
    for at, wait in loads:
        wait()
        qkv_ref[at, :] = (dot(rows_ref[at, :], weight_ref[...]) + bias_ref[...]).astype(LOW)
    outs += moves([(qkv_ref, qkv_out)], move_sem, n_parts + 1)
    for h in range(heads):
        lo = h * HD
        queries = qkv_ref[:, lo : lo + HD]
        keys = qkv_ref[:, cols + lo : cols + lo + HD]
        values = qkv_ref[:, 2 * cols + lo : 2 * cols + lo + HD]
        scores = dot(keys, queries, NT)
        highest = jnp.max(scores, axis=0, keepdims=True)
        probs = jnp.exp2((scores - highest) * SCALE_LOG2)
        total = jnp.sum(probs, axis=0, keepdims=True)
        mixed = dot(values.T, probs.astype(LOW)) / total
        lse_ref[h : h + 1, :] = highest * SCALE_LOG2 + jnp.log2(total)
        mixed_ref[:, lo : lo + HD] = mixed.T.astype(LOW)
    for wait in outs:
        wait()


def kernel_call(body, name, n_vmem, n_any, weight, out_shape, out_any, flops, transcendentals, scratch, n_moves):
    sources, count = weight.sources, weight.count
    shape = sources[0].shape
    moved = sum(math.prod(o.shape) * o.dtype.itemsize for o in out_shape) + 2 * count * shape[1] * shape[2]
    anywhere, inside = pl.BlockSpec(memory_space=pl.ANY), pl.BlockSpec(memory_space=pltpu.VMEM)
    return pl.pallas_call(
        functools.partial(body, count, shape[0]),
        in_specs=[pl.BlockSpec(memory_space=pltpu.SMEM)] + [inside] * n_vmem + [anywhere] * (n_any + len(sources)),
        out_specs=[anywhere if n in out_any else inside for n in range(len(out_shape))],
        out_shape=out_shape,
        scratch_shapes=[
            *(pltpu.VMEM(of.shape, of.dtype) for of in scratch),
            pltpu.SemaphoreType.DMA((count,)),
            pltpu.SemaphoreType.DMA((n_moves,)),
        ],
        compiler_params=pltpu.CompilerParams(vmem_limit_bytes=VMEM_LIMIT),
        cost_estimate=pl.CostEstimate(flops=flops, bytes_accessed=moved, transcendentals=transcendentals),
        name=name,
    )


class Weight:
    def __init__(self, sources, table):
        images, n_dp = table.shape
        _, rows, cols = sources[0].shape
        self.width = n_dp * rows
        if rows % 16:
            whole = jnp.take(jnp.concatenate(sources, axis=0), table.reshape(-1), axis=0)
            sources = (whole.reshape(images, self.width, cols),)
            table = jnp.arange(images, dtype=jnp.int32)[:, None]
        self.sources, self.table, self.count, self.cols = sources, table, table.shape[1], cols
        self.shape = jax.ShapeDtypeStruct((self.width, cols), LOW)


def attend_forward(bias, parts, weight, i, heads):
    cols = heads * HD
    qkv = jax.ShapeDtypeStruct((LEN, 3 * cols), LOW)
    rows = jax.ShapeDtypeStruct((LEN, weight.width), LOW)
    return kernel_call(
        functools.partial(attend_forward_body, heads, len(parts)),
        "attend_forward",
        1,
        len(parts),
        weight,
        [qkv, jax.ShapeDtypeStruct((LEN, cols), LOW), jax.ShapeDtypeStruct((heads, LEN), F32), weight.shape],
        (0, 3),
        heads * LEN * LEN * 1536 + 2 * LEN * weight.width * 3 * cols,
        heads * LEN * LEN,
        [qkv, weight.shape, rows],
        len(parts) + 2,
    )(weight.table[i], bias, *parts, *weight.sources)


def place_body(count, first, table_ref, *refs):
    sources, (weight_ref, sem, _) = refs[:-3], refs[-3:]
    start_pieces(count, first, table_ref, sources, weight_ref, sem)()


def placed(weight, enter, i, name):
    return kernel_call(place_body, name, 0, 0, weight, [weight.shape], (), 0, 0, (), 1)(
        enter(weight.table[i]), *weight.sources
    )[0]


def in_steps(at):
    half = at.size // 2
    return pl.ds(at.start, half), pl.ds(at.start + half, half)


def up_body(n_parts, count, first, table_ref, bias_ref, *refs):
    parts, sources = refs[:n_parts], refs[n_parts:-9]
    act_out, slope_out, weight_out, act_ref, slope_ref, weight_ref, rows_ref, sem, move_sem = refs[-9:]
    wait_pieces = start_pieces(count, first, table_ref, sources, weight_ref, sem)
    loads = load_parts(parts, rows_ref, move_sem)
    wait_pieces()
    outs = moves([(weight_ref, weight_out)], move_sem, n_parts)
    for n, (whole, wait) in enumerate(loads):
        wait()
        for at in in_steps(whole):
            u = dot(rows_ref[at, :], weight_ref[...]) + bias_ref[...]
            square = u * u
            bend = jnp.tanh(u * (GELU_A + GELU_A * GELU_B * square))
            half = 0.5 + 0.5 * bend
            act_ref[at, :] = (u * half).astype(LOW)
            inner = u * (GELU_A + 3 * GELU_A * GELU_B * square)
            slope_ref[at, :] = (half + 0.5 * inner * (1 - bend * bend)).astype(LOW)
        outs += moves(
            [(act_ref.at[whole], act_out.at[whole]), (slope_ref.at[whole], slope_out.at[whole])],
            move_sem,
            n_parts + 1 + 2 * n,
        )
    for wait in outs:
        wait()


def up(bias, parts, weight, i):
    hidden = jax.ShapeDtypeStruct((LEN, weight.cols), LOW)
    rows = jax.ShapeDtypeStruct((LEN, weight.width), LOW)
    return kernel_call(
        functools.partial(up_body, len(parts)), "up", 1, len(parts), weight, [hidden, hidden, weight.shape], (0, 1, 2),
        2 * LEN * weight.width * weight.cols, LEN * weight.cols, [hidden, hidden, weight.shape, rows],
        3 * len(parts) + 1,
    )(weight.table[i], bias, *parts, *weight.sources)


def pre_grad_body(n_parts, count, first, table_ref, slope_in, *refs):
    parts, sources = refs[:n_parts], refs[n_parts:-9]
    grad_out, bias_ref, weight_out, grad_ref, slope_ref, weight_ref, rows_ref, sem, move_sem = refs[-9:]
    wait_pieces = start_pieces(count, first, table_ref, sources, weight_ref, sem)
    loads = load_parts(parts, rows_ref, move_sem)
    slopes = moves([(slope_in.at[at], slope_ref.at[at]) for at, _ in loads], move_sem, n_parts)
    bias_ref[...] = jnp.zeros_like(bias_ref)
    wait_pieces()
    outs = moves([(weight_ref, weight_out)], move_sem, 2 * n_parts)
    for n, (whole, wait) in enumerate(loads):
        wait()
        slopes[n]()
        for at in in_steps(whole):
            grad = (dot(rows_ref[at, :], weight_ref[...]) * slope_ref[at, :].astype(F32)).astype(LOW)
            grad_ref[at, :] = grad
            bias_ref[...] += jnp.sum(grad.astype(F32), axis=0, keepdims=True)
        outs += moves([(grad_ref.at[whole], grad_out.at[whole])], move_sem, 2 * n_parts + 1 + n)
    for wait in outs:
        wait()


def pre_grad(table, slope, parts, weight):
    hidden = jax.ShapeDtypeStruct((LEN, weight.cols), LOW)
    rows = jax.ShapeDtypeStruct((LEN, weight.width), LOW)
    return kernel_call(
        functools.partial(pre_grad_body, len(parts)), "pre_grad", 0, 1 + len(parts), weight,
        [hidden, jax.ShapeDtypeStruct((1, weight.cols), F32), weight.shape], (0, 2),
        2 * LEN * weight.width * weight.cols, 0, [hidden, hidden, weight.shape, rows],
        3 * len(parts) + 1,
    )(table, slope, *parts, *weight.sources)


def attend_backward_body(heads, lse_ref, qkv_in, mixed_in, out_in, *refs):
    parts, (grads_ref, grad_ref, qkv_ref, mixed_ref, out_ref, rows_ref, move_sem) = refs[:-7], refs[-7:]
    cols = heads * HD
    loads = load_parts(parts, rows_ref, move_sem)
    wait_out, wait_qkv, wait_mixed = moves(
        [(out_in, out_ref), (qkv_in, qkv_ref), (mixed_in, mixed_ref)], move_sem, len(parts)
    )
    wait_out()
    for at, wait in loads:
        wait()
        grad_ref[at, :] = dot(rows_ref[at, :], out_ref[...]).astype(LOW)
    wait_qkv()
    wait_mixed()
    for h in range(heads):
        lo = h * HD
        queries = qkv_ref[:, lo : lo + HD]
        keys = qkv_ref[:, cols + lo : cols + lo + HD]
        values = qkv_ref[:, 2 * cols + lo : 2 * cols + lo + HD]
        grads = grad_ref[:, lo : lo + HD]
        products = grads.astype(F32) * mixed_ref[:, lo : lo + HD].astype(F32)
        delta = jnp.sum(products.T, axis=0, keepdims=True)
        probs = jnp.exp2(dot(keys, queries, NT) * SCALE_LOG2 - lse_ref[h : h + 1, :])
        prob_grad = dot(values, grads, NT)
        grads_ref[:, 2 * cols + lo : 2 * cols + lo + HD] = dot(probs.astype(LOW), grads).astype(LOW)
        score_grad = (probs * (prob_grad - delta)).astype(LOW)
        grads_ref[:, cols + lo : cols + lo + HD] = (dot(score_grad, queries) * SCALE).astype(LOW)
        grads_ref[:, lo : lo + HD] = (dot(keys.T, score_grad) * SCALE).T.astype(LOW)


def attend_backward(lse, qkv, mixed, out_full, parts, heads):
    rows, cols = mixed.shape
    return pl.pallas_call(
        functools.partial(attend_backward_body, heads),
        in_specs=[pl.BlockSpec(memory_space=pltpu.VMEM)] + [pl.BlockSpec(memory_space=pl.ANY)] * (3 + len(parts)),
        out_specs=pl.BlockSpec(memory_space=pltpu.VMEM),
        out_shape=jax.ShapeDtypeStruct((rows, 3 * cols), LOW),
        scratch_shapes=[
            pltpu.VMEM((rows, cols), LOW),
            pltpu.VMEM(qkv.shape, LOW),
            pltpu.VMEM(mixed.shape, LOW),
            pltpu.VMEM(out_full.shape, LOW),
            pltpu.VMEM((rows, out_full.shape[0]), LOW),
            pltpu.SemaphoreType.DMA((3 + len(parts),)),
        ],
        compiler_params=pltpu.CompilerParams(vmem_limit_bytes=VMEM_LIMIT),
        cost_estimate=SHORT,
        name="attend_backward",
    )(lse, qkv, mixed, out_full, *parts)


def weight_grad_body(images, n_dp, half, table_ref, *refs):
    lefts, rights, (keep_ref, send_ref, turned, product, sem) = refs[: -5 - images], refs[-5 - images : -5], refs[-5:]
    width = turned.shape[0]
    shard_rows = width // n_dp
    for left, at in spans(lefts):
        turned[:, at] = left[...].T
    step = width // 2

    def piece(start, n):
        slot = table_ref[n]
        source = product.at[n // n_dp, pl.ds((n % n_dp) * shard_rows, shard_rows)]
        for out_ref, mine, index in ((keep_ref, slot < half, slot), (send_ref, slot >= half, slot - half)):
            @pl.when(mine)
            def _():
                copy = pltpu.make_async_copy(source, out_ref.at[index], sem.at[n])
                if start:
                    copy.start()
                else:
                    copy.wait()

    for i in range(images):
        for part in range(2):
            at = pl.ds(part * step, step)
            product[i, at, :] = dot(turned[at, :], rights[i][...]).astype(LOW)
            for d in range(part * n_dp // 2, (part + 1) * n_dp // 2):
                piece(True, i * n_dp + d)
    for n in range(images * n_dp):
        piece(False, n)


def weight_grad(table, lefts, rights, n_dp, name):
    images = len(rights)
    rows, width = LEN, lefts[0].shape[1]
    cols = rights[0].shape[1]
    shard_rows = width // n_dp
    half = images * n_dp // 2
    if shard_rows % 16:
        left = jnp.concatenate(lefts, axis=0)
        whole = jnp.concatenate([dot(left, right, TN).astype(LOW) for right in rights], axis=0)
        slots = whole.reshape(images * n_dp, shard_rows, cols)
        order = jnp.zeros_like(table).at[table].set(jnp.arange(table.shape[0], dtype=jnp.int32))
        slots = jnp.take(slots, order, axis=0)
        return slots[:half], slots[half:]
    shape = jax.ShapeDtypeStruct((half, shard_rows, cols), LOW)
    return pl.pallas_call(
        functools.partial(weight_grad_body, images, n_dp, half),
        in_specs=[pl.BlockSpec(memory_space=pltpu.SMEM)] + [pl.BlockSpec(memory_space=pltpu.VMEM)] * (len(lefts) + images),
        out_specs=[pl.BlockSpec(memory_space=pl.ANY)] * 2,
        out_shape=[shape, shape],
        scratch_shapes=[
            pltpu.VMEM((width, rows), LOW),
            pltpu.VMEM((images, width, cols), LOW),
            pltpu.SemaphoreType.DMA((images * n_dp,)),
        ],
        compiler_params=pltpu.CompilerParams(vmem_limit_bytes=VMEM_LIMIT),
        cost_estimate=SHORT,
        name=name,
    )(table, *lefts, *rights)


class Plan:
    def __init__(self, n_dp, n_t, ranks):
        self.n_dp, self.n_t, self.ranks = n_dp, n_t, ranks
        self.images = n_t // ranks
        dims = [("dp", 1 << b) for b in reversed(range(n_dp.bit_length() - 1))]
        image_dims = [("image", 1 << b) for b in reversed(range(self.images.bit_length() - 1))]
        even = dims + image_dims
        odd = list(even)
        if image_dims and dims:
            odd[-2], odd[-1] = odd[-1], odd[-2]
        self.orders = {"far": (even, odd), "near": tuple(way[-2:-1] + way[:-2] + way[-1:] for way in (even, odd))}
        self.stages = len(even)
        self.rank_stages = ranks.bit_length() - 1

    def permute(self, values, partner):
        pairs = []
        for d in range(self.n_dp):
            for t in range(self.n_t):
                d2, i2, r2 = partner(d, t // self.ranks, t % self.ranks)
                pairs.append((d * self.n_t + t, d2 * self.n_t + i2 * self.ranks + r2))
        return lax.ppermute(values, ("dp", "tensor"), pairs)

    def exchange(self, values, stage, way="far"):
        def partner(d, i, r):
            kind, step = self.orders[way][r & 1][stage]
            return (d ^ step, i, r) if kind == "dp" else (d, i ^ step, r)

        return self.permute(values, partner)

    def rank_exchange(self, values, stage):
        return self.permute(values, lambda d, i, r: (d, i, r ^ (1 << stage)))

    def slots(self, way="far"):
        me_dp, me_t = lax.axis_index("dp"), lax.axis_index("tensor")
        flips = jnp.arange(self.n_dp, dtype=jnp.int32)[None, :] ^ me_dp
        images = jnp.arange(self.images, dtype=jnp.int32)[:, None]

        def table(order):
            total = jnp.zeros((self.images, self.n_dp), jnp.int32)
            for stage, (kind, step) in enumerate(order):
                source = flips if kind == "dp" else images
                total = total + jnp.where((source & step) != 0, 1 << stage, 0)
            return total

        even, odd = self.orders[way]
        return jnp.where((me_t % self.ranks) & 1, table(odd), table(even))

    def rank_gather(self, shard):
        parts = [shard]
        for stage in range(self.rank_stages):
            mine = jnp.concatenate(parts, axis=0) if stage else shard
            parts.append(self.rank_exchange(mine, stage))
        return parts

    def rank_scatter(self, rows, *after):
        for stage in reversed(range(self.rank_stages)):
            half = rows.shape[0] // 2
            (theirs,) = tie((self.rank_exchange(rows[half:].astype(LOW), stage),), after)
            rows = rows[:half] + theirs.astype(F32)
        return rows


class Gather:
    def __init__(self, plan, order, shard, way="far"):
        self.plan, self.order, self.held, self.stage, self.way = plan, order, (shard[None],), 0, way

    def to(self, stage, *after):
        while self.stage < stage:
            held = tie(self.held, [*self.order.done, *after])
            mine = held[0] if len(held) == 1 else jnp.concatenate(held, axis=0)
            self.held = (mine, self.plan.exchange(mine, self.stage, self.way))
            self.order.begun.append(mine)
            self.stage += 1
        return self.held[-1]

    def weight(self):
        self.to(self.plan.stages)
        return Weight(self.held, self.plan.slots(self.way))


class Scatter:
    def __init__(self, plan, order, keep, send, way):
        self.plan, self.order, self.keep, self.send, self.way = plan, order, keep, send, way
        self.theirs, self.stage = None, plan.stages

    def total(self, part):
        return self.keep[part].astype(F32) + self.theirs[part].astype(F32)

    def to(self, stage, *after):
        while self.stage > stage:
            if self.theirs is not None:
                self.keep, self.theirs = tie((self.keep, self.theirs), [*self.order.done, *after])
                half = self.keep.shape[0] // 2
                self.send, self.keep = self.total(slice(half, None)).astype(LOW), self.total(slice(half)).astype(LOW)
            self.stage -= 1
            self.theirs = self.plan.exchange(self.send, self.stage, self.way)
            self.order.begun.append(self.send)
        return self.theirs

    def finish(self):
        self.to(0)
        return self.total(0)


def local(
    tokens, gain_one, shift_one, w_query, b_query, w_key, w_value, b_value, w_out, b_out,
    gain_two, shift_two, w_up, b_up, w_down, b_down, cotangent, plan=None,
):
    images, ranks, n_dp = plan.images, plan.ranks, plan.n_dp
    shard_rows = w_query.shape[0]
    width = tokens.shape[1]
    head_cols, hidden_cols = w_query.shape[1], w_up.shape[1]
    heads = head_cols // HD
    me_t = lax.axis_index("tensor")
    me_image, me_rank = me_t // ranks, me_t % ranks

    def shard_of(i):
        return (me_image ^ i) * ranks + me_rank

    def columns(vector, cols):
        return [lax.dynamic_slice_in_dim(vector, shard_of(i) * cols, cols) for i in range(images)]

    def uncolumns(parts, length):
        cols = parts[0].shape[0]
        blank = jnp.zeros((length,), F32)
        for i in range(images):
            blank = lax.dynamic_update_slice_in_dim(blank, parts[i], shard_of(i) * cols, 0)
        return blank

    order = Order()

    def scatter(lefts, rights, name, way="far"):
        table = plan.slots(way).reshape(-1)
        keep, send = weight_grad(order.enter(table), lefts, rights, n_dp, name)
        order.leave(send)
        begun = Scatter(plan, order, keep, send, way)
        begun.to(plan.stages - 1)
        return begun

    def low(values):
        return values.astype(LOW)

    each = range(images)
    last, near = plan.stages, max(plan.stages - 1, 0)
    far = max(plan.stages - 2, 0)
    first = max(plan.stages - 3, 0)
    gather_qkv = Gather(plan, order, jnp.concatenate([low(w_query), low(w_key), low(w_value)], axis=1))
    gather_out = Gather(plan, order, low(w_out).T)
    gather_up = Gather(plan, order, low(w_up))
    gather_down = Gather(plan, order, low(w_down).T, "near")
    cot_rows = plan.rank_gather(cotangent)
    inputs32 = tokens.astype(F32)
    normed_one = low(layer_norm(inputs32, gain_one, shift_one))
    rows_one = plan.rank_gather(normed_one)
    token = gather_qkv.to(first)
    down_token = gather_down.to(min(1, far))
    gather_qkv.to(far)
    out_token = gather_out.to(first, token)
    token = gather_qkv.held[-1]
    gather_qkv.to(near, out_token, down_token, rows_one[-1], cot_rows[-1])
    up_token = gather_up.to(first, token)
    out_token = gather_out.to(far, token)
    token = gather_qkv.held[-1]
    gather_qkv.to(last, out_token, up_token)
    gather_up.to(far, token)
    gather_out.to(near, gather_qkv.held[-1])
    gather_up.to(near, gather_qkv.held[-1])
    gather_down.to(near - 1, gather_up.held[0])
    order.begun = [gather_up.held[0], gather_down.held[0]]

    query_bias, value_bias = columns(b_query, head_cols), columns(b_value, head_cols)
    blank = jnp.zeros((head_cols,), F32)
    qkv, mixed, lse, qkv_full = [None] * images, [None] * images, [None] * images, [None] * images
    for i in each:
        bias = order.enter(jnp.concatenate([query_bias[i], blank, value_bias[i]])[None])
        qkv[i], mixed[i], lse[i], qkv_full[i] = attend_forward(bias, rows_one, gather_qkv.weight(), i, heads)
        order.leave(lse[i])
        if i == 0:
            gather_out.to(last)
            gather_up.to(last)
            gather_down.to(near)
    gather_down.to(last)

    out_full = [placed(gather_out.weight(), order.enter, i, "place_out") for i in each]
    down_held = [] if gather_down.stage < last else [gather_down.held[0]]
    attn = sum(dot(mixed[i], out_full[i], NT) for i in each)
    (attn,) = tie((attn,), down_held)
    residual = inputs32 + plan.rank_scatter(attn, gather_up.held[-1]) + b_out
    normed_two = low(layer_norm(residual, gain_two, shift_two))
    order.leave(normed_two[:8])
    rows_two = plan.rank_gather(normed_two)
    up_bias = columns(b_up, hidden_cols)
    act, slope, up_full = [None] * images, [None] * images, [None] * images
    for i in each:
        bias = order.enter(up_bias[i][None])
        act[i], slope[i], up_full[i] = up(bias, rows_two, gather_up.weight(), i)
        order.leave(act[i])
    scatter_down = scatter(cot_rows, act, "grad_down", "near")

    grad_out = cotangent.astype(F32)
    down_bias_grad = jnp.sum(grad_out, axis=0)
    pre_low, up_bias_parts, down_full = [None] * images, [None] * images, [None] * images
    down_weight = gather_down.weight()
    for i in each:
        table = order.enter(down_weight.table[i])
        pre_low[i], up_bias_parts[i], down_full[i] = pre_grad(table, slope[i], cot_rows, down_weight)
        order.leave(up_bias_parts[i])
    partial_two = sum(dot(pre_low[i], up_full[i], NT) for i in each)
    order.leave(partial_two[:8])
    scatter_up = scatter(rows_two, pre_low, "grad_up")
    scatter_down.to(far)
    (partial_two,) = tie((partial_two,), [scatter_down.send])
    norm_two_grad = plan.rank_scatter(partial_two)
    _, pull_two = jax.vjp(layer_norm, residual, gain_two, shift_two)
    residual_part, gain_two_grad, shift_two_grad = pull_two(norm_two_grad)
    residual_grad = grad_out + residual_part
    branch_low = low(residual_grad)
    out_bias_grad = jnp.sum(branch_low, axis=0, dtype=F32)
    branch_rows = plan.rank_gather(branch_low)
    scatter_out = scatter(branch_rows, mixed, "grad_out")

    qkv_grads = []
    for i in each:
        start = order.enter(lse[i])
        qkv_grads.append(attend_backward(start, qkv[i], mixed[i], out_full[i], branch_rows, heads))
        order.leave(qkv_grads[i])
        if i == 0:
            scatter_down.to(first)
            scatter_up.to(far)
            scatter_out.to(far)
    scatter_qkv = scatter(rows_one, qkv_grads, "grad_qkv")
    scatter_up.to(first)
    scatter_out.to(first)
    scatter_down.to(0)
    partial_one = sum(dot(order.enter(qkv_grads[i]), qkv_full[i], NT) for i in each)
    order.leave(partial_one[:8])
    mlp = sum(dot(order.enter(act[i]), down_full[i], NT) for i in each)
    order.leave(mlp[:8])
    scatter_up.to(0)
    scatter_out.to(0)
    norm_one_grad = order.enter(plan.rank_scatter(partial_one))
    _, pull_one = jax.vjp(layer_norm, inputs32, gain_one, shift_one)
    input_part, gain_one_grad, shift_one_grad = pull_one(norm_one_grad)
    grad_tokens = low(residual_grad + input_part)
    output = low(residual + plan.rank_scatter(mlp) + b_down)
    order.leave(gain_one_grad)
    scatter_qkv.to(far)
    gain_one_grad = order.enter(gain_one_grad)
    down_grad = scatter_down.finish().T
    up_grad = scatter_up.finish()
    out_grad = scatter_out.finish().T
    qkv_sums = [jnp.sum(grads, axis=0, dtype=F32) for grads in qkv_grads]
    up_bias_grad = uncolumns([order.enter(part)[0] for part in up_bias_parts], b_up.shape[0])
    query_bias_grad = uncolumns([sums[:head_cols] for sums in qkv_sums], b_query.shape[0])
    value_bias_grad = uncolumns([sums[2 * head_cols :] for sums in qkv_sums], b_value.shape[0])

    vectors = [
        gain_one_grad, shift_one_grad, query_bias_grad, value_bias_grad, out_bias_grad,
        gain_two_grad, shift_two_grad, up_bias_grad, down_bias_grad,
    ]
    lengths = [vector.shape[0] for vector in vectors]
    together = jnp.concatenate([*vectors, jnp.zeros((-sum(lengths) % 1024,), F32)])
    for stage in range(plan.rank_stages):
        together = together + plan.rank_exchange(together, stage)
    for stage in range(plan.stages):
        together = together + plan.exchange(together, stage)
        if stage in (first, near):
            order.leave(together)
            if stage == first:
                scatter_qkv.to(first, up_grad, out_grad)
            else:
                scatter_qkv.to(0)
            together = order.enter(together)
    qkv_grad = scatter_qkv.finish()
    query_grad, key_grad, value_grad = (qkv_grad[:, n * head_cols : (n + 1) * head_cols] for n in range(3))
    small, begin = [], 0
    for length in lengths:
        small.append(together[begin : begin + length])
        begin += length
    return (
        output, grad_tokens, small[0], small[1], query_grad, small[2], key_grad, value_grad, small[3],
        out_grad, small[4], small[5], small[6], up_grad, small[7], down_grad, small[8],
    )


def solution(mesh):
    split = P(("dp", "tensor"), None)
    whole, wide, tall = P(), P("dp", "tensor"), P("tensor", "dp")
    n_dp, n_t = mesh.shape["dp"], mesh.shape["tensor"]

    def layer(*args):
        rows = args[0].shape[0] // (n_dp * n_t)
        plan = Plan(n_dp, n_t, LEN // rows)
        return jax.shard_map(
            functools.partial(local, plan=plan),
            mesh=mesh,
            in_specs=(
                split, whole, whole, wide, whole, wide, wide, whole, tall, whole,
                whole, whole, wide, whole, tall, whole, split,
            ),
            out_specs=(
                split, split, whole, whole, wide, whole, wide, wide, whole,
                tall, whole, whole, whole, wide, whole, tall, whole,
            ),
            check_vma=False,
        )(*args)

    return layer
```

```python
import functools
import math

import jax
import jax.numpy as jnp
from jax import lax
from jax.experimental import pallas as pl
from jax.experimental.pallas import tpu as pltpu
from jax.sharding import PartitionSpec as P

HD = 72
LEN = 1024
NORM_EPS = 1e-06
LOW = jnp.bfloat16
F32 = jnp.float32
SCALE = HD ** (-0.5)
SCALE_LOG2 = SCALE * math.log2(math.e)
VMEM_LIMIT = 50 * 1024 * 1024
GELU_A = math.sqrt(2 / math.pi)
GELU_B = 0.044715
SHORT = pl.CostEstimate(flops=0, bytes_accessed=0, transcendentals=0)

NN = (((1,), (0,)), ((), ()))
NT = (((1,), (1,)), ((), ()))
TN = (((0,), (0,)), ((), ()))


def dot(left, right, dims=NN):
    return lax.dot_general(left, right, dims, preferred_element_type=F32)


def layer_norm(values, norm_gain, norm_shift):
    centred = values - jnp.mean(values, axis=-1, keepdims=True)
    spread = jnp.mean(centred * centred, axis=-1, keepdims=True)
    return centred * lax.rsqrt(spread + NORM_EPS) * norm_gain + norm_shift


def tie(values, others):
    if not others:
        return values
    return lax.optimization_barrier((*values, *others))[: len(values)]


class Order:
    def __init__(self):
        self.done, self.begun = [], []

    def enter(self, operand):
        return tie((operand,), [*self.done, *self.begun])[0]

    def leave(self, result):
        self.done, self.begun = [result], []


def start_pieces(count, first, table_ref, sources, target_ref, sem):
    rows = target_ref.shape[0] // count

    def each(start):
        for n in range(count):
            slot = table_ref[n]
            for at, source in enumerate(sources):
                @pl.when((slot >= at * first) & (slot < (at + 1) * first))
                def _():
                    copy = pltpu.make_async_copy(
                        source.at[slot - at * first], target_ref.at[pl.ds(n * rows, rows)], sem.at[n]
                    )
                    if start:
                        copy.start()
                    else:
                        copy.wait()

    each(True)
    return functools.partial(each, False)


def spans(parts):
    begin = 0
    for part in parts:
        yield part, pl.ds(begin, part.shape[0])
        begin += part.shape[0]


def moves(pairs, sem, first=0):
    copies = [pltpu.make_async_copy(source, to, sem.at[first + n]) for n, (source, to) in enumerate(pairs)]
    for copy in copies:
        copy.start()
    return [copy.wait for copy in copies]


def load_parts(parts, rows_ref, sem):
    places = [at for _, at in spans(parts)]
    return list(zip(places, moves([(part, rows_ref.at[at]) for part, at in zip(parts, places)], sem)))


def attend_forward_body(heads, n_parts, count, first, table_ref, bias_ref, *refs):
    parts, sources = refs[:n_parts], refs[n_parts:-9]
    qkv_out, mixed_ref, lse_ref, weight_out, qkv_ref, weight_ref, rows_ref, sem, move_sem = refs[-9:]
    wait_pieces = start_pieces(count, first, table_ref, sources, weight_ref, sem)
    loads = load_parts(parts, rows_ref, move_sem)
    cols = heads * HD
    wait_pieces()
    outs = moves([(weight_ref, weight_out)], move_sem, n_parts)
    for at, wait in loads:
        wait()
        qkv_ref[at, :] = (dot(rows_ref[at, :], weight_ref[...]) + bias_ref[...]).astype(LOW)
    outs += moves([(qkv_ref, qkv_out)], move_sem, n_parts + 1)
    for h in range(heads):
        lo = h * HD
        queries = qkv_ref[:, lo : lo + HD]
        keys = qkv_ref[:, cols + lo : cols + lo + HD]
        values = qkv_ref[:, 2 * cols + lo : 2 * cols + lo + HD]
        scores = dot(keys, queries, NT)
        highest = jnp.max(scores, axis=0, keepdims=True)
        probs = jnp.exp2((scores - highest) * SCALE_LOG2)
        total = jnp.sum(probs, axis=0, keepdims=True)
        mixed = dot(values.T, probs.astype(LOW)) / total
        lse_ref[h : h + 1, :] = highest * SCALE_LOG2 + jnp.log2(total)
        mixed_ref[:, lo : lo + HD] = mixed.T.astype(LOW)
    for wait in outs:
        wait()


def kernel_call(body, name, n_vmem, n_any, weight, out_shape, out_any, flops, transcendentals, scratch, n_moves):
    sources, count = weight.sources, weight.count
    shape = sources[0].shape
    moved = sum(math.prod(o.shape) * o.dtype.itemsize for o in out_shape) + 2 * count * shape[1] * shape[2]
    anywhere, inside = pl.BlockSpec(memory_space=pl.ANY), pl.BlockSpec(memory_space=pltpu.VMEM)
    return pl.pallas_call(
        functools.partial(body, count, shape[0]),
        in_specs=[pl.BlockSpec(memory_space=pltpu.SMEM)] + [inside] * n_vmem + [anywhere] * (n_any + len(sources)),
        out_specs=[anywhere if n in out_any else inside for n in range(len(out_shape))],
        out_shape=out_shape,
        scratch_shapes=[
            *(pltpu.VMEM(of.shape, of.dtype) for of in scratch),
            pltpu.SemaphoreType.DMA((count,)),
            pltpu.SemaphoreType.DMA((n_moves,)),
        ],
        compiler_params=pltpu.CompilerParams(vmem_limit_bytes=VMEM_LIMIT),
        cost_estimate=pl.CostEstimate(flops=flops, bytes_accessed=moved, transcendentals=transcendentals),
        name=name,
    )


class Weight:
    def __init__(self, sources, table):
        images, n_dp = table.shape
        _, rows, cols = sources[0].shape
        self.width = n_dp * rows
        if rows % 16:
            whole = jnp.take(jnp.concatenate(sources, axis=0), table.reshape(-1), axis=0)
            sources = (whole.reshape(images, self.width, cols),)
            table = jnp.arange(images, dtype=jnp.int32)[:, None]
        self.sources, self.table, self.count, self.cols = sources, table, table.shape[1], cols
        self.shape = jax.ShapeDtypeStruct((self.width, cols), LOW)


def attend_forward(bias, parts, weight, i, heads):
    cols = heads * HD
    qkv = jax.ShapeDtypeStruct((LEN, 3 * cols), LOW)
    rows = jax.ShapeDtypeStruct((LEN, weight.width), LOW)
    return kernel_call(
        functools.partial(attend_forward_body, heads, len(parts)),
        "attend_forward",
        1,
        len(parts),
        weight,
        [qkv, jax.ShapeDtypeStruct((LEN, cols), LOW), jax.ShapeDtypeStruct((heads, LEN), F32), weight.shape],
        (0, 3),
        heads * LEN * LEN * 1536 + 2 * LEN * weight.width * 3 * cols,
        heads * LEN * LEN,
        [qkv, weight.shape, rows],
        len(parts) + 2,
    )(weight.table[i], bias, *parts, *weight.sources)


def place_body(count, first, table_ref, *refs):
    sources, (weight_ref, sem, _) = refs[:-3], refs[-3:]
    start_pieces(count, first, table_ref, sources, weight_ref, sem)()


def placed(weight, enter, i, name):
    return kernel_call(place_body, name, 0, 0, weight, [weight.shape], (), 0, 0, (), 1)(
        enter(weight.table[i]), *weight.sources
    )[0]


def in_steps(at):
    half = at.size // 2
    return pl.ds(at.start, half), pl.ds(at.start + half, half)


def up_body(n_parts, count, first, table_ref, bias_ref, *refs):
    parts, sources = refs[:n_parts], refs[n_parts:-9]
    act_out, slope_out, weight_out, act_ref, slope_ref, weight_ref, rows_ref, sem, move_sem = refs[-9:]
    wait_pieces = start_pieces(count, first, table_ref, sources, weight_ref, sem)
    loads = load_parts(parts, rows_ref, move_sem)
    wait_pieces()
    outs = moves([(weight_ref, weight_out)], move_sem, n_parts)
    for n, (whole, wait) in enumerate(loads):
        wait()
        for at in in_steps(whole):
            u = dot(rows_ref[at, :], weight_ref[...]) + bias_ref[...]
            square = u * u
            bend = jnp.tanh(u * (GELU_A + GELU_A * GELU_B * square))
            half = 0.5 + 0.5 * bend
            act_ref[at, :] = (u * half).astype(LOW)
            inner = u * (GELU_A + 3 * GELU_A * GELU_B * square)
            slope_ref[at, :] = (half + 0.5 * inner * (1 - bend * bend)).astype(LOW)
        outs += moves(
            [(act_ref.at[whole], act_out.at[whole]), (slope_ref.at[whole], slope_out.at[whole])],
            move_sem,
            n_parts + 1 + 2 * n,
        )
    for wait in outs:
        wait()


def up(bias, parts, weight, i):
    hidden = jax.ShapeDtypeStruct((LEN, weight.cols), LOW)
    rows = jax.ShapeDtypeStruct((LEN, weight.width), LOW)
    return kernel_call(
        functools.partial(up_body, len(parts)), "up", 1, len(parts), weight, [hidden, hidden, weight.shape], (0, 1, 2),
        2 * LEN * weight.width * weight.cols, LEN * weight.cols, [hidden, hidden, weight.shape, rows],
        3 * len(parts) + 1,
    )(weight.table[i], bias, *parts, *weight.sources)


def pre_grad_body(n_parts, count, first, table_ref, slope_in, *refs):
    parts, sources = refs[:n_parts], refs[n_parts:-9]
    grad_out, bias_ref, weight_out, grad_ref, slope_ref, weight_ref, rows_ref, sem, move_sem = refs[-9:]
    wait_pieces = start_pieces(count, first, table_ref, sources, weight_ref, sem)
    loads = load_parts(parts, rows_ref, move_sem)
    slopes = moves([(slope_in.at[at], slope_ref.at[at]) for at, _ in loads], move_sem, n_parts)
    bias_ref[...] = jnp.zeros_like(bias_ref)
    wait_pieces()
    outs = moves([(weight_ref, weight_out)], move_sem, 2 * n_parts)
    for n, (whole, wait) in enumerate(loads):
        wait()
        slopes[n]()
        for at in in_steps(whole):
            grad = (dot(rows_ref[at, :], weight_ref[...]) * slope_ref[at, :].astype(F32)).astype(LOW)
            grad_ref[at, :] = grad
            bias_ref[...] += jnp.sum(grad.astype(F32), axis=0, keepdims=True)
        outs += moves([(grad_ref.at[whole], grad_out.at[whole])], move_sem, 2 * n_parts + 1 + n)
    for wait in outs:
        wait()


def pre_grad(table, slope, parts, weight):
    hidden = jax.ShapeDtypeStruct((LEN, weight.cols), LOW)
    rows = jax.ShapeDtypeStruct((LEN, weight.width), LOW)
    return kernel_call(
        functools.partial(pre_grad_body, len(parts)), "pre_grad", 0, 1 + len(parts), weight,
        [hidden, jax.ShapeDtypeStruct((1, weight.cols), F32), weight.shape], (0, 2),
        2 * LEN * weight.width * weight.cols, 0, [hidden, hidden, weight.shape, rows],
        3 * len(parts) + 1,
    )(table, slope, *parts, *weight.sources)


def attend_backward_body(heads, lse_ref, qkv_in, mixed_in, out_in, *refs):
    parts, (grads_ref, grad_ref, qkv_ref, mixed_ref, out_ref, rows_ref, move_sem) = refs[:-7], refs[-7:]
    cols = heads * HD
    loads = load_parts(parts, rows_ref, move_sem)
    wait_out, wait_qkv, wait_mixed = moves(
        [(out_in, out_ref), (qkv_in, qkv_ref), (mixed_in, mixed_ref)], move_sem, len(parts)
    )
    wait_out()
    for at, wait in loads:
        wait()
        grad_ref[at, :] = dot(rows_ref[at, :], out_ref[...]).astype(LOW)
    wait_qkv()
    wait_mixed()
    for h in range(heads):
        lo = h * HD
        queries = qkv_ref[:, lo : lo + HD]
        keys = qkv_ref[:, cols + lo : cols + lo + HD]
        values = qkv_ref[:, 2 * cols + lo : 2 * cols + lo + HD]
        grads = grad_ref[:, lo : lo + HD]
        products = grads.astype(F32) * mixed_ref[:, lo : lo + HD].astype(F32)
        delta = jnp.sum(products.T, axis=0, keepdims=True)
        probs = jnp.exp2(dot(keys, queries, NT) * SCALE_LOG2 - lse_ref[h : h + 1, :])
        prob_grad = dot(values, grads, NT)
        grads_ref[:, 2 * cols + lo : 2 * cols + lo + HD] = dot(probs.astype(LOW), grads).astype(LOW)
        score_grad = (probs * (prob_grad - delta)).astype(LOW)
        grads_ref[:, cols + lo : cols + lo + HD] = (dot(score_grad, queries) * SCALE).astype(LOW)
        grads_ref[:, lo : lo + HD] = (dot(keys.T, score_grad) * SCALE).T.astype(LOW)


def attend_backward(lse, qkv, mixed, out_full, parts, heads):
    rows, cols = mixed.shape
    return pl.pallas_call(
        functools.partial(attend_backward_body, heads),
        in_specs=[pl.BlockSpec(memory_space=pltpu.VMEM)] + [pl.BlockSpec(memory_space=pl.ANY)] * (3 + len(parts)),
        out_specs=pl.BlockSpec(memory_space=pltpu.VMEM),
        out_shape=jax.ShapeDtypeStruct((rows, 3 * cols), LOW),
        scratch_shapes=[
            pltpu.VMEM((rows, cols), LOW),
            pltpu.VMEM(qkv.shape, LOW),
            pltpu.VMEM(mixed.shape, LOW),
            pltpu.VMEM(out_full.shape, LOW),
            pltpu.VMEM((rows, out_full.shape[0]), LOW),
            pltpu.SemaphoreType.DMA((3 + len(parts),)),
        ],
        compiler_params=pltpu.CompilerParams(vmem_limit_bytes=VMEM_LIMIT),
        cost_estimate=SHORT,
        name="attend_backward",
    )(lse, qkv, mixed, out_full, *parts)


def weight_grad_body(images, n_dp, half, table_ref, *refs):
    lefts, rights, (keep_ref, send_ref, turned, product, sem) = refs[: -5 - images], refs[-5 - images : -5], refs[-5:]
    width = turned.shape[0]
    shard_rows = width // n_dp
    for left, at in spans(lefts):
        turned[:, at] = left[...].T
    step = width // 2

    def piece(start, n):
        slot = table_ref[n]
        source = product.at[n // n_dp, pl.ds((n % n_dp) * shard_rows, shard_rows)]
        for out_ref, mine, index in ((keep_ref, slot < half, slot), (send_ref, slot >= half, slot - half)):
            @pl.when(mine)
            def _():
                copy = pltpu.make_async_copy(source, out_ref.at[index], sem.at[n])
                if start:
                    copy.start()
                else:
                    copy.wait()

    for i in range(images):
        for part in range(2):
            at = pl.ds(part * step, step)
            product[i, at, :] = dot(turned[at, :], rights[i][...]).astype(LOW)
            for d in range(part * n_dp // 2, (part + 1) * n_dp // 2):
                piece(True, i * n_dp + d)
    for n in range(images * n_dp):
        piece(False, n)


def weight_grad(table, lefts, rights, n_dp, name):
    images = len(rights)
    rows, width = LEN, lefts[0].shape[1]
    cols = rights[0].shape[1]
    shard_rows = width // n_dp
    half = images * n_dp // 2
    if shard_rows % 16:
        left = jnp.concatenate(lefts, axis=0)
        whole = jnp.concatenate([dot(left, right, TN).astype(LOW) for right in rights], axis=0)
        slots = whole.reshape(images * n_dp, shard_rows, cols)
        order = jnp.zeros_like(table).at[table].set(jnp.arange(table.shape[0], dtype=jnp.int32))
        slots = jnp.take(slots, order, axis=0)
        return slots[:half], slots[half:]
    shape = jax.ShapeDtypeStruct((half, shard_rows, cols), LOW)
    return pl.pallas_call(
        functools.partial(weight_grad_body, images, n_dp, half),
        in_specs=[pl.BlockSpec(memory_space=pltpu.SMEM)] + [pl.BlockSpec(memory_space=pltpu.VMEM)] * (len(lefts) + images),
        out_specs=[pl.BlockSpec(memory_space=pl.ANY)] * 2,
        out_shape=[shape, shape],
        scratch_shapes=[
            pltpu.VMEM((width, rows), LOW),
            pltpu.VMEM((images, width, cols), LOW),
            pltpu.SemaphoreType.DMA((images * n_dp,)),
        ],
        compiler_params=pltpu.CompilerParams(vmem_limit_bytes=VMEM_LIMIT),
        cost_estimate=SHORT,
        name=name,
    )(table, *lefts, *rights)


class Plan:
    def __init__(self, n_dp, n_t, ranks):
        self.n_dp, self.n_t, self.ranks = n_dp, n_t, ranks
        self.images = n_t // ranks
        dims = [("dp", 1 << b) for b in reversed(range(n_dp.bit_length() - 1))]
        image_dims = [("image", 1 << b) for b in reversed(range(self.images.bit_length() - 1))]
        even = dims + image_dims
        odd = list(even)
        if image_dims and dims:
            odd[-2], odd[-1] = odd[-1], odd[-2]
        self.orders = {"far": (even, odd), "near": tuple(way[-2:-1] + way[:-2] + way[-1:] for way in (even, odd))}
        self.stages = len(even)
        self.rank_stages = ranks.bit_length() - 1

    def permute(self, values, partner):
        pairs = []
        for d in range(self.n_dp):
            for t in range(self.n_t):
                d2, i2, r2 = partner(d, t // self.ranks, t % self.ranks)
                pairs.append((d * self.n_t + t, d2 * self.n_t + i2 * self.ranks + r2))
        return lax.ppermute(values, ("dp", "tensor"), pairs)

    def exchange(self, values, stage, way="far"):
        def partner(d, i, r):
            kind, step = self.orders[way][r & 1][stage]
            return (d ^ step, i, r) if kind == "dp" else (d, i ^ step, r)

        return self.permute(values, partner)

    def rank_exchange(self, values, stage):
        return self.permute(values, lambda d, i, r: (d, i, r ^ (1 << stage)))

    def slots(self, way="far"):
        me_dp, me_t = lax.axis_index("dp"), lax.axis_index("tensor")
        flips = jnp.arange(self.n_dp, dtype=jnp.int32)[None, :] ^ me_dp
        images = jnp.arange(self.images, dtype=jnp.int32)[:, None]

        def table(order):
            total = jnp.zeros((self.images, self.n_dp), jnp.int32)
            for stage, (kind, step) in enumerate(order):
                source = flips if kind == "dp" else images
                total = total + jnp.where((source & step) != 0, 1 << stage, 0)
            return total

        even, odd = self.orders[way]
        return jnp.where((me_t % self.ranks) & 1, table(odd), table(even))

    def rank_gather(self, shard):
        parts = [shard]
        for stage in range(self.rank_stages):
            mine = jnp.concatenate(parts, axis=0) if stage else shard
            parts.append(self.rank_exchange(mine, stage))
        return parts

    def rank_scatter(self, rows, *after):
        for stage in reversed(range(self.rank_stages)):
            half = rows.shape[0] // 2
            (theirs,) = tie((self.rank_exchange(rows[half:].astype(LOW), stage),), after)
            rows = rows[:half] + theirs.astype(F32)
        return rows


class Gather:
    def __init__(self, plan, order, shard, way="far", joined=True):
        self.plan, self.order, self.held, self.stage, self.way = plan, order, (shard[None],), 0, way
        self.joined = joined

    def to(self, stage, *after):
        while self.stage < stage:
            held = tie(self.held, [*self.order.done, *after])
            if len(held) > 1 and (self.joined or self.stage < self.plan.stages - 1):
                held = (jnp.concatenate(held, axis=0),)
            self.held = (*held, *(self.plan.exchange(mine, self.stage, self.way) for mine in held))
            self.order.begun.append(held[0])
            self.stage += 1
        return self.held[-1]

    def weight(self):
        self.to(self.plan.stages)
        return Weight(self.held, self.plan.slots(self.way))


class Scatter:
    def __init__(self, plan, order, keep, send, way):
        self.plan, self.order, self.keep, self.send, self.way = plan, order, keep, send, way
        self.theirs, self.stage = None, plan.stages

    def total(self, part):
        return self.keep[part].astype(F32) + self.theirs[part].astype(F32)

    def to(self, stage, *after):
        while self.stage > stage:
            if self.theirs is not None:
                self.keep, self.theirs = tie((self.keep, self.theirs), [*self.order.done, *after])
                half = self.keep.shape[0] // 2
                self.send, self.keep = self.total(slice(half, None)).astype(LOW), self.total(slice(half)).astype(LOW)
            self.stage -= 1
            self.theirs = self.plan.exchange(self.send, self.stage, self.way)
            self.order.begun.append(self.send)
        return self.theirs

    def finish(self, *after):
        self.to(0)
        self.keep, self.theirs = tie((self.keep, self.theirs), after)
        return self.total(0)


def local(
    tokens, gain_one, shift_one, w_query, b_query, w_key, w_value, b_value, w_out, b_out,
    gain_two, shift_two, w_up, b_up, w_down, b_down, cotangent, plan=None,
):
    images, ranks, n_dp = plan.images, plan.ranks, plan.n_dp
    shard_rows = w_query.shape[0]
    width = tokens.shape[1]
    head_cols, hidden_cols = w_query.shape[1], w_up.shape[1]
    heads = head_cols // HD
    me_t = lax.axis_index("tensor")
    me_image, me_rank = me_t // ranks, me_t % ranks

    def shard_of(i):
        return (me_image ^ i) * ranks + me_rank

    def columns(vector, cols):
        return [lax.dynamic_slice_in_dim(vector, shard_of(i) * cols, cols) for i in range(images)]

    def uncolumns(parts, length):
        cols = parts[0].shape[0]
        blank = jnp.zeros((length,), F32)
        for i in range(images):
            blank = lax.dynamic_update_slice_in_dim(blank, parts[i], shard_of(i) * cols, 0)
        return blank

    order = Order()

    def scatter(lefts, rights, name, way="far"):
        table = plan.slots(way).reshape(-1)
        keep, send = weight_grad(order.enter(table), lefts, rights, n_dp, name)
        order.leave(send)
        begun = Scatter(plan, order, keep, send, way)
        begun.to(plan.stages - 1)
        return begun

    def low(values):
        return values.astype(LOW)

    each = range(images)
    last, near = plan.stages, max(plan.stages - 1, 0)
    far = max(plan.stages - 2, 0)
    first = max(plan.stages - 3, 0)
    gather_qkv = Gather(plan, order, jnp.concatenate([low(w_query), low(w_key), low(w_value)], axis=1))
    gather_out = Gather(plan, order, low(w_out).T)
    gather_up = Gather(plan, order, low(w_up))
    gather_down = Gather(plan, order, low(w_down).T, "near", joined=False)
    cot_rows = plan.rank_gather(cotangent)
    inputs32 = tokens.astype(F32)
    normed_one = low(layer_norm(inputs32, gain_one, shift_one))
    rows_one = plan.rank_gather(normed_one)
    token = gather_qkv.to(first)
    down_token = gather_down.to(min(1, far))
    gather_qkv.to(far)
    out_token = gather_out.to(first, token)
    token = gather_qkv.held[-1]
    gather_qkv.to(near, out_token, down_token, rows_one[-1], cot_rows[-1])
    up_token = gather_up.to(first, token)
    out_token = gather_out.to(far, token)
    token = gather_qkv.held[-1]
    gather_qkv.to(last, out_token, up_token)
    gather_up.to(far, token)
    gather_out.to(near, gather_qkv.held[-1])
    gather_up.to(near, gather_qkv.held[-1])
    gather_down.to(near - 1, gather_up.held[0])
    order.begun = [gather_up.held[0], gather_down.held[0]]

    query_bias, value_bias = columns(b_query, head_cols), columns(b_value, head_cols)
    blank = jnp.zeros((head_cols,), F32)
    qkv, mixed, lse, qkv_full = [None] * images, [None] * images, [None] * images, [None] * images
    for i in each:
        bias = order.enter(jnp.concatenate([query_bias[i], blank, value_bias[i]])[None])
        qkv[i], mixed[i], lse[i], qkv_full[i] = attend_forward(bias, rows_one, gather_qkv.weight(), i, heads)
        order.leave(lse[i])
        if i == 0:
            gather_out.to(last)
            gather_up.to(last)
            gather_down.to(near)

    out_full = [placed(gather_out.weight(), order.enter, i, "place_out") for i in each]
    attn = sum(dot(mixed[i], out_full[i], NT) for i in each)
    order.leave(attn[:8])
    gather_down.to(last)
    (attn,) = tie((order.enter(attn),), [gather_up.held[-1]])
    residual = inputs32 + plan.rank_scatter(attn) + b_out
    normed_two = low(layer_norm(residual, gain_two, shift_two))
    order.leave(normed_two[:8])
    rows_two = plan.rank_gather(normed_two)
    up_bias = columns(b_up, hidden_cols)
    act, slope, up_full = [None] * images, [None] * images, [None] * images
    for i in each:
        bias = order.enter(up_bias[i][None])
        act[i], slope[i], up_full[i] = up(bias, rows_two, gather_up.weight(), i)
        order.leave(act[i])
    scatter_down = scatter(cot_rows, act, "grad_down", "near")

    grad_out = cotangent.astype(F32)
    down_bias_grad = jnp.sum(grad_out, axis=0)
    pre_low, up_bias_parts, down_full = [None] * images, [None] * images, [None] * images
    down_weight = gather_down.weight()
    for i in each:
        table = order.enter(down_weight.table[i])
        pre_low[i], up_bias_parts[i], down_full[i] = pre_grad(table, slope[i], cot_rows, down_weight)
        order.leave(up_bias_parts[i])
    partial_two = sum(dot(pre_low[i], up_full[i], NT) for i in each)
    order.leave(partial_two[:8])
    scatter_up = scatter(rows_two, pre_low, "grad_up")
    scatter_down.to(far)
    (partial_two,) = tie((partial_two,), [scatter_down.send])
    norm_two_grad = plan.rank_scatter(partial_two)
    _, pull_two = jax.vjp(layer_norm, residual, gain_two, shift_two)
    residual_part, gain_two_grad, shift_two_grad = pull_two(norm_two_grad)
    residual_grad = grad_out + residual_part
    branch_low = low(residual_grad)
    out_bias_grad = jnp.sum(branch_low, axis=0, dtype=F32)
    branch_rows = plan.rank_gather(branch_low)
    scatter_out = scatter(branch_rows, mixed, "grad_out")

    qkv_grads = []
    for i in each:
        start = order.enter(lse[i])
        qkv_grads.append(attend_backward(start, qkv[i], mixed[i], out_full[i], branch_rows, heads))
        order.leave(qkv_grads[i])
        if i == 0:
            scatter_down.to(first)
            scatter_up.to(far)
            scatter_out.to(far)
    scatter_qkv = scatter(rows_one, qkv_grads, "grad_qkv")
    scatter_up.to(first)
    scatter_out.to(first)
    scatter_down.to(0)
    partial_one = sum(dot(order.enter(qkv_grads[i]), qkv_full[i], NT) for i in each)
    order.leave(partial_one[:8])
    down_grad = scatter_down.finish(*order.done)
    order.begun.append(down_grad)
    mlp = sum(dot(order.enter(act[i]), down_full[i], NT) for i in each)
    order.leave(mlp[:8])
    scatter_up.to(0)
    scatter_out.to(0)
    mlp = plan.rank_scatter(mlp)
    (norm_one_grad,) = tie((order.enter(plan.rank_scatter(partial_one)),), [mlp])
    _, pull_one = jax.vjp(layer_norm, inputs32, gain_one, shift_one)
    input_part, gain_one_grad, shift_one_grad = pull_one(norm_one_grad)
    grad_tokens = low(residual_grad + input_part)
    output = low(residual + mlp + b_down)
    order.leave(gain_one_grad)
    scatter_qkv.to(far)
    up_grad = scatter_up.finish()
    out_grad = scatter_out.finish().T
    down_grad = down_grad.T
    gain_one_grad = order.enter(gain_one_grad)
    qkv_sums = [jnp.sum(grads, axis=0, dtype=F32) for grads in qkv_grads]
    up_bias_grad = uncolumns([order.enter(part)[0] for part in up_bias_parts], b_up.shape[0])
    query_bias_grad = uncolumns([sums[:head_cols] for sums in qkv_sums], b_query.shape[0])
    value_bias_grad = uncolumns([sums[2 * head_cols :] for sums in qkv_sums], b_value.shape[0])

    vectors = [
        gain_one_grad, shift_one_grad, query_bias_grad, value_bias_grad, out_bias_grad,
        gain_two_grad, shift_two_grad, up_bias_grad, down_bias_grad,
    ]
    lengths = [vector.shape[0] for vector in vectors]
    together = jnp.concatenate([*vectors, jnp.zeros((-sum(lengths) % 1024,), F32)])
    for stage in range(plan.rank_stages):
        together = together + plan.rank_exchange(together, stage)
    for stage in range(plan.stages):
        together = together + plan.exchange(together, stage)
        if stage in (first - 1, first):
            order.leave(together)
            if stage == first - 1:
                scatter_qkv.to(first, up_grad, out_grad)
            else:
                scatter_qkv.to(0)
            together = order.enter(together)
    qkv_grad = scatter_qkv.finish()
    query_grad, key_grad, value_grad = (qkv_grad[:, n * head_cols : (n + 1) * head_cols] for n in range(3))
    small, begin = [], 0
    for length in lengths:
        small.append(together[begin : begin + length])
        begin += length
    return (
        output, grad_tokens, small[0], small[1], query_grad, small[2], key_grad, value_grad, small[3],
        out_grad, small[4], small[5], small[6], up_grad, small[7], down_grad, small[8],
    )


def solution(mesh):
    split = P(("dp", "tensor"), None)
    whole, wide, tall = P(), P("dp", "tensor"), P("tensor", "dp")
    n_dp, n_t = mesh.shape["dp"], mesh.shape["tensor"]

    def layer(*args):
        rows = args[0].shape[0] // (n_dp * n_t)
        plan = Plan(n_dp, n_t, LEN // rows)
        return jax.shard_map(
            functools.partial(local, plan=plan),
            mesh=mesh,
            in_specs=(
                split, whole, whole, wide, whole, wide, wide, whole, tall, whole,
                whole, whole, wide, whole, tall, whole, split,
            ),
            out_specs=(
                split, split, whole, whole, wide, whole, wide, wide, whole,
                tall, whole, whole, whole, wide, whole, tall, whole,
            ),
            check_vma=False,
        )(*args)

    return layer
```

```python
import functools
import math

import jax
import jax.numpy as jnp
from jax import lax
from jax.experimental import pallas as pl
from jax.experimental.pallas import tpu as pltpu
from jax.sharding import PartitionSpec as P

HD = 72
LEN = 1024
NORM_EPS = 1e-06
LOW = jnp.bfloat16
F32 = jnp.float32
SCALE = HD ** (-0.5)
SCALE_LOG2 = SCALE * math.log2(math.e)
VMEM_LIMIT = 50 * 1024 * 1024
GELU_A = math.sqrt(2 / math.pi)
GELU_B = 0.044715
SHORT = pl.CostEstimate(flops=0, bytes_accessed=0, transcendentals=0)

NN = (((1,), (0,)), ((), ()))
NT = (((1,), (1,)), ((), ()))
TN = (((0,), (0,)), ((), ()))


def dot(left, right, dims=NN):
    return lax.dot_general(left, right, dims, preferred_element_type=F32)


def layer_norm(values, norm_gain, norm_shift):
    centred = values - jnp.mean(values, axis=-1, keepdims=True)
    spread = jnp.mean(centred * centred, axis=-1, keepdims=True)
    return centred * lax.rsqrt(spread + NORM_EPS) * norm_gain + norm_shift


def tie(values, others):
    if not others:
        return values
    return lax.optimization_barrier((*values, *others))[: len(values)]


class Order:
    def __init__(self):
        self.done, self.begun = [], []

    def enter(self, operand):
        return tie((operand,), [*self.done, *self.begun])[0]

    def leave(self, result):
        self.done, self.begun = [result], []


def start_pieces(count, first, table_ref, sources, target_ref, sem):
    rows = target_ref.shape[0] // count

    def each(start):
        for n in range(count):
            slot = table_ref[n]
            for at, source in enumerate(sources):
                @pl.when((slot >= at * first) & (slot < (at + 1) * first))
                def _():
                    copy = pltpu.make_async_copy(
                        source.at[slot - at * first], target_ref.at[pl.ds(n * rows, rows)], sem.at[n]
                    )
                    if start:
                        copy.start()
                    else:
                        copy.wait()

    each(True)
    return functools.partial(each, False)


def spans(parts):
    begin = 0
    for part in parts:
        yield part, pl.ds(begin, part.shape[0])
        begin += part.shape[0]


def moves(pairs, sem, first=0):
    copies = [pltpu.make_async_copy(source, to, sem.at[first + n]) for n, (source, to) in enumerate(pairs)]
    for copy in copies:
        copy.start()
    return [copy.wait for copy in copies]


def load_parts(parts, rows_ref, sem):
    places = [at for _, at in spans(parts)]
    return list(zip(places, moves([(part, rows_ref.at[at]) for part, at in zip(parts, places)], sem)))


def attend_forward_body(heads, n_parts, count, first, table_ref, bias_ref, *refs):
    parts, sources = refs[:n_parts], refs[n_parts:-9]
    qkv_out, mixed_ref, lse_ref, weight_out, qkv_ref, weight_ref, rows_ref, sem, move_sem = refs[-9:]
    wait_pieces = start_pieces(count, first, table_ref, sources, weight_ref, sem)
    loads = load_parts(parts, rows_ref, move_sem)
    cols = heads * HD
    wait_pieces()
    outs = moves([(weight_ref, weight_out)], move_sem, n_parts)
    for at, wait in loads:
        wait()
        qkv_ref[at, :] = (dot(rows_ref[at, :], weight_ref[...]) + bias_ref[...]).astype(LOW)
    outs += moves([(qkv_ref, qkv_out)], move_sem, n_parts + 1)
    for h in range(heads):
        lo = h * HD
        queries = qkv_ref[:, lo : lo + HD]
        keys = qkv_ref[:, cols + lo : cols + lo + HD]
        values = qkv_ref[:, 2 * cols + lo : 2 * cols + lo + HD]
        scores = dot(keys, queries, NT)
        highest = jnp.max(scores, axis=0, keepdims=True)
        probs = jnp.exp2((scores - highest) * SCALE_LOG2)
        total = jnp.sum(probs, axis=0, keepdims=True)
        mixed = dot(values.T, probs.astype(LOW)) / total
        lse_ref[h : h + 1, :] = highest * SCALE_LOG2 + jnp.log2(total)
        mixed_ref[:, lo : lo + HD] = mixed.T.astype(LOW)
    for wait in outs:
        wait()


def kernel_call(body, name, n_vmem, n_any, weight, out_shape, out_any, flops, transcendentals, scratch, n_moves):
    sources, count = weight.sources, weight.count
    shape = sources[0].shape
    moved = sum(math.prod(o.shape) * o.dtype.itemsize for o in out_shape) + 2 * count * shape[1] * shape[2]
    anywhere, inside = pl.BlockSpec(memory_space=pl.ANY), pl.BlockSpec(memory_space=pltpu.VMEM)
    return pl.pallas_call(
        functools.partial(body, count, shape[0]),
        in_specs=[pl.BlockSpec(memory_space=pltpu.SMEM)] + [inside] * n_vmem + [anywhere] * (n_any + len(sources)),
        out_specs=[anywhere if n in out_any else inside for n in range(len(out_shape))],
        out_shape=out_shape,
        scratch_shapes=[
            *(pltpu.VMEM(of.shape, of.dtype) for of in scratch),
            pltpu.SemaphoreType.DMA((count,)),
            pltpu.SemaphoreType.DMA((n_moves,)),
        ],
        compiler_params=pltpu.CompilerParams(vmem_limit_bytes=VMEM_LIMIT),
        cost_estimate=pl.CostEstimate(flops=flops, bytes_accessed=moved, transcendentals=transcendentals),
        name=name,
    )


class Weight:
    def __init__(self, sources, table):
        images, n_dp = table.shape
        _, rows, cols = sources[0].shape
        self.width = n_dp * rows
        if rows % 16:
            whole = jnp.take(jnp.concatenate(sources, axis=0), table.reshape(-1), axis=0)
            sources = (whole.reshape(images, self.width, cols),)
            table = jnp.arange(images, dtype=jnp.int32)[:, None]
        self.sources, self.table, self.count, self.cols = sources, table, table.shape[1], cols
        self.shape = jax.ShapeDtypeStruct((self.width, cols), LOW)


def attend_forward(bias, parts, weight, i, heads):
    cols = heads * HD
    qkv = jax.ShapeDtypeStruct((LEN, 3 * cols), LOW)
    rows = jax.ShapeDtypeStruct((LEN, weight.width), LOW)
    return kernel_call(
        functools.partial(attend_forward_body, heads, len(parts)),
        "attend_forward",
        1,
        len(parts),
        weight,
        [qkv, jax.ShapeDtypeStruct((LEN, cols), LOW), jax.ShapeDtypeStruct((heads, LEN), F32), weight.shape],
        (0, 3),
        heads * LEN * LEN * 1536 + 2 * LEN * weight.width * 3 * cols,
        heads * LEN * LEN,
        [qkv, weight.shape, rows],
        len(parts) + 2,
    )(weight.table[i], bias, *parts, *weight.sources)


def place_body(count, first, table_ref, *refs):
    sources, (weight_ref, sem, _) = refs[:-3], refs[-3:]
    start_pieces(count, first, table_ref, sources, weight_ref, sem)()


def placed(weight, enter, i, name):
    return kernel_call(place_body, name, 0, 0, weight, [weight.shape], (), 0, 0, (), 1)(
        enter(weight.table[i]), *weight.sources
    )[0]


def in_steps(at):
    half = at.size // 2
    return pl.ds(at.start, half), pl.ds(at.start + half, half)


def up_body(n_parts, count, first, table_ref, bias_ref, *refs):
    parts, sources = refs[:n_parts], refs[n_parts:-9]
    act_out, slope_out, weight_out, act_ref, slope_ref, weight_ref, rows_ref, sem, move_sem = refs[-9:]
    wait_pieces = start_pieces(count, first, table_ref, sources, weight_ref, sem)
    loads = load_parts(parts, rows_ref, move_sem)
    wait_pieces()
    outs = moves([(weight_ref, weight_out)], move_sem, n_parts)
    for n, (whole, wait) in enumerate(loads):
        wait()
        for at in in_steps(whole):
            u = dot(rows_ref[at, :], weight_ref[...]) + bias_ref[...]
            square = u * u
            bend = jnp.tanh(u * (GELU_A + GELU_A * GELU_B * square))
            half = 0.5 + 0.5 * bend
            act_ref[at, :] = (u * half).astype(LOW)
            inner = u * (GELU_A + 3 * GELU_A * GELU_B * square)
            slope_ref[at, :] = (half + 0.5 * inner * (1 - bend * bend)).astype(LOW)
        outs += moves(
            [(act_ref.at[whole], act_out.at[whole]), (slope_ref.at[whole], slope_out.at[whole])],
            move_sem,
            n_parts + 1 + 2 * n,
        )
    for wait in outs:
        wait()


def up(bias, parts, weight, i):
    hidden = jax.ShapeDtypeStruct((LEN, weight.cols), LOW)
    rows = jax.ShapeDtypeStruct((LEN, weight.width), LOW)
    return kernel_call(
        functools.partial(up_body, len(parts)), "up", 1, len(parts), weight, [hidden, hidden, weight.shape], (0, 1, 2),
        2 * LEN * weight.width * weight.cols, LEN * weight.cols, [hidden, hidden, weight.shape, rows],
        3 * len(parts) + 1,
    )(weight.table[i], bias, *parts, *weight.sources)


def pre_grad_body(n_parts, count, first, table_ref, slope_in, *refs):
    parts, sources = refs[:n_parts], refs[n_parts:-9]
    grad_out, bias_ref, weight_out, grad_ref, slope_ref, weight_ref, rows_ref, sem, move_sem = refs[-9:]
    wait_pieces = start_pieces(count, first, table_ref, sources, weight_ref, sem)
    loads = load_parts(parts, rows_ref, move_sem)
    slopes = moves([(slope_in.at[at], slope_ref.at[at]) for at, _ in loads], move_sem, n_parts)
    bias_ref[...] = jnp.zeros_like(bias_ref)
    wait_pieces()
    outs = moves([(weight_ref, weight_out)], move_sem, 2 * n_parts)
    for n, (whole, wait) in enumerate(loads):
        wait()
        slopes[n]()
        for at in in_steps(whole):
            grad = (dot(rows_ref[at, :], weight_ref[...]) * slope_ref[at, :].astype(F32)).astype(LOW)
            grad_ref[at, :] = grad
            bias_ref[...] += jnp.sum(grad.astype(F32), axis=0, keepdims=True)
        outs += moves([(grad_ref.at[whole], grad_out.at[whole])], move_sem, 2 * n_parts + 1 + n)
    for wait in outs:
        wait()


def pre_grad(table, slope, parts, weight):
    hidden = jax.ShapeDtypeStruct((LEN, weight.cols), LOW)
    rows = jax.ShapeDtypeStruct((LEN, weight.width), LOW)
    return kernel_call(
        functools.partial(pre_grad_body, len(parts)), "pre_grad", 0, 1 + len(parts), weight,
        [hidden, jax.ShapeDtypeStruct((1, weight.cols), F32), weight.shape], (0, 2),
        2 * LEN * weight.width * weight.cols, 0, [hidden, hidden, weight.shape, rows],
        3 * len(parts) + 1,
    )(table, slope, *parts, *weight.sources)


def attend_backward_body(heads, lse_ref, qkv_in, mixed_in, out_in, *refs):
    parts, (grads_ref, grad_ref, qkv_ref, mixed_ref, out_ref, rows_ref, move_sem) = refs[:-7], refs[-7:]
    cols = heads * HD
    loads = load_parts(parts, rows_ref, move_sem)
    wait_out, wait_qkv, wait_mixed = moves(
        [(out_in, out_ref), (qkv_in, qkv_ref), (mixed_in, mixed_ref)], move_sem, len(parts)
    )
    wait_out()
    for at, wait in loads:
        wait()
        grad_ref[at, :] = dot(rows_ref[at, :], out_ref[...]).astype(LOW)
    wait_qkv()
    wait_mixed()
    for h in range(heads):
        lo = h * HD
        queries = qkv_ref[:, lo : lo + HD]
        keys = qkv_ref[:, cols + lo : cols + lo + HD]
        values = qkv_ref[:, 2 * cols + lo : 2 * cols + lo + HD]
        grads = grad_ref[:, lo : lo + HD]
        products = grads.astype(F32) * mixed_ref[:, lo : lo + HD].astype(F32)
        delta = jnp.sum(products.T, axis=0, keepdims=True)
        probs = jnp.exp2(dot(keys, queries, NT) * SCALE_LOG2 - lse_ref[h : h + 1, :])
        prob_grad = dot(values, grads, NT)
        grads_ref[:, 2 * cols + lo : 2 * cols + lo + HD] = dot(probs.astype(LOW), grads).astype(LOW)
        score_grad = (probs * (prob_grad - delta)).astype(LOW)
        grads_ref[:, cols + lo : cols + lo + HD] = (dot(score_grad, queries) * SCALE).astype(LOW)
        grads_ref[:, lo : lo + HD] = (dot(keys.T, score_grad) * SCALE).T.astype(LOW)


def attend_backward(lse, qkv, mixed, out_full, parts, heads):
    rows, cols = mixed.shape
    return pl.pallas_call(
        functools.partial(attend_backward_body, heads),
        in_specs=[pl.BlockSpec(memory_space=pltpu.VMEM)] + [pl.BlockSpec(memory_space=pl.ANY)] * (3 + len(parts)),
        out_specs=pl.BlockSpec(memory_space=pltpu.VMEM),
        out_shape=jax.ShapeDtypeStruct((rows, 3 * cols), LOW),
        scratch_shapes=[
            pltpu.VMEM((rows, cols), LOW),
            pltpu.VMEM(qkv.shape, LOW),
            pltpu.VMEM(mixed.shape, LOW),
            pltpu.VMEM(out_full.shape, LOW),
            pltpu.VMEM((rows, out_full.shape[0]), LOW),
            pltpu.SemaphoreType.DMA((3 + len(parts),)),
        ],
        compiler_params=pltpu.CompilerParams(vmem_limit_bytes=VMEM_LIMIT),
        cost_estimate=SHORT,
        name="attend_backward",
    )(lse, qkv, mixed, out_full, *parts)


def weight_grad_body(images, n_dp, half, table_ref, *refs):
    lefts, rights, (keep_ref, send_ref, turned, product, sem) = refs[: -5 - images], refs[-5 - images : -5], refs[-5:]
    width = turned.shape[0]
    shard_rows = width // n_dp
    for left, at in spans(lefts):
        turned[:, at] = left[...].T
    step = width // 2

    def piece(start, n):
        slot = table_ref[n]
        source = product.at[n // n_dp, pl.ds((n % n_dp) * shard_rows, shard_rows)]
        for out_ref, mine, index in ((keep_ref, slot < half, slot), (send_ref, slot >= half, slot - half)):
            @pl.when(mine)
            def _():
                copy = pltpu.make_async_copy(source, out_ref.at[index], sem.at[n])
                if start:
                    copy.start()
                else:
                    copy.wait()

    for i in range(images):
        for part in range(2):
            at = pl.ds(part * step, step)
            product[i, at, :] = dot(turned[at, :], rights[i][...]).astype(LOW)
            for d in range(part * n_dp // 2, (part + 1) * n_dp // 2):
                piece(True, i * n_dp + d)
    for n in range(images * n_dp):
        piece(False, n)


def weight_grad(table, lefts, rights, n_dp, name):
    images = len(rights)
    rows, width = LEN, lefts[0].shape[1]
    cols = rights[0].shape[1]
    shard_rows = width // n_dp
    half = images * n_dp // 2
    if shard_rows % 16:
        left = jnp.concatenate(lefts, axis=0)
        whole = jnp.concatenate([dot(left, right, TN).astype(LOW) for right in rights], axis=0)
        slots = whole.reshape(images * n_dp, shard_rows, cols)
        order = jnp.zeros_like(table).at[table].set(jnp.arange(table.shape[0], dtype=jnp.int32))
        slots = jnp.take(slots, order, axis=0)
        return slots[:half], slots[half:]
    shape = jax.ShapeDtypeStruct((half, shard_rows, cols), LOW)
    return pl.pallas_call(
        functools.partial(weight_grad_body, images, n_dp, half),
        in_specs=[pl.BlockSpec(memory_space=pltpu.SMEM)] + [pl.BlockSpec(memory_space=pltpu.VMEM)] * (len(lefts) + images),
        out_specs=[pl.BlockSpec(memory_space=pl.ANY)] * 2,
        out_shape=[shape, shape],
        scratch_shapes=[
            pltpu.VMEM((width, rows), LOW),
            pltpu.VMEM((images, width, cols), LOW),
            pltpu.SemaphoreType.DMA((images * n_dp,)),
        ],
        compiler_params=pltpu.CompilerParams(vmem_limit_bytes=VMEM_LIMIT),
        cost_estimate=SHORT,
        name=name,
    )(table, *lefts, *rights)


class Plan:
    def __init__(self, n_dp, n_t, ranks):
        self.n_dp, self.n_t, self.ranks = n_dp, n_t, ranks
        self.images = n_t // ranks
        dims = [("dp", 1 << b) for b in reversed(range(n_dp.bit_length() - 1))]
        image_dims = [("image", 1 << b) for b in reversed(range(self.images.bit_length() - 1))]
        even = dims + image_dims
        odd = list(even)
        if image_dims and dims:
            odd[-2], odd[-1] = odd[-1], odd[-2]
        self.orders = {"far": (even, odd), "near": tuple(way[-2:-1] + way[:-2] + way[-1:] for way in (even, odd))}
        self.stages = len(even)
        self.rank_stages = ranks.bit_length() - 1

    def permute(self, values, partner):
        pairs = []
        for d in range(self.n_dp):
            for t in range(self.n_t):
                d2, i2, r2 = partner(d, t // self.ranks, t % self.ranks)
                pairs.append((d * self.n_t + t, d2 * self.n_t + i2 * self.ranks + r2))
        return lax.ppermute(values, ("dp", "tensor"), pairs)

    def exchange(self, values, stage, way="far"):
        def partner(d, i, r):
            kind, step = self.orders[way][r & 1][stage]
            return (d ^ step, i, r) if kind == "dp" else (d, i ^ step, r)

        return self.permute(values, partner)

    def rank_exchange(self, values, stage):
        return self.permute(values, lambda d, i, r: (d, i, r ^ (1 << stage)))

    def slots(self, way="far"):
        me_dp, me_t = lax.axis_index("dp"), lax.axis_index("tensor")
        flips = jnp.arange(self.n_dp, dtype=jnp.int32)[None, :] ^ me_dp
        images = jnp.arange(self.images, dtype=jnp.int32)[:, None]

        def table(order):
            total = jnp.zeros((self.images, self.n_dp), jnp.int32)
            for stage, (kind, step) in enumerate(order):
                source = flips if kind == "dp" else images
                total = total + jnp.where((source & step) != 0, 1 << stage, 0)
            return total

        even, odd = self.orders[way]
        return jnp.where((me_t % self.ranks) & 1, table(odd), table(even))

    def rank_gather(self, shard):
        parts = [shard]
        for stage in range(self.rank_stages):
            mine = jnp.concatenate(parts, axis=0) if stage else shard
            parts.append(self.rank_exchange(mine, stage))
        return parts

    def rank_scatter(self, rows, *after):
        for stage in reversed(range(self.rank_stages)):
            half = rows.shape[0] // 2
            (theirs,) = tie((self.rank_exchange(rows[half:].astype(LOW), stage),), after)
            rows = rows[:half] + theirs.astype(F32)
        return rows


class Gather:
    def __init__(self, plan, order, shard, way="far", joined=True):
        self.plan, self.order, self.held, self.stage, self.way = plan, order, (shard[None],), 0, way
        self.joined = joined

    def to(self, stage, *after):
        while self.stage < stage:
            held = tie(self.held, [*self.order.done, *after])
            if len(held) > 1 and (self.joined or self.stage < self.plan.stages - 1):
                held = (jnp.concatenate(held, axis=0),)
            self.held = (*held, *(self.plan.exchange(mine, self.stage, self.way) for mine in held))
            self.order.begun.append(held[0])
            self.stage += 1
        return self.held[-1]

    def weight(self):
        self.to(self.plan.stages)
        return Weight(self.held, self.plan.slots(self.way))


class Scatter:
    def __init__(self, plan, order, keep, send, way):
        self.plan, self.order, self.keep, self.send, self.way = plan, order, keep, send, way
        self.theirs, self.stage = None, plan.stages

    def total(self, part):
        return self.keep[part].astype(F32) + self.theirs[part].astype(F32)

    def to(self, stage, *after):
        while self.stage > stage:
            if self.theirs is not None:
                self.keep, self.theirs = tie((self.keep, self.theirs), [*self.order.done, *after])
                half = self.keep.shape[0] // 2
                self.send, self.keep = self.total(slice(half, None)).astype(LOW), self.total(slice(half)).astype(LOW)
            self.stage -= 1
            self.theirs = self.plan.exchange(self.send, self.stage, self.way)
            self.order.begun.append(self.send)
        return self.theirs

    def finish(self, *after):
        self.to(0)
        self.keep, self.theirs = tie((self.keep, self.theirs), after)
        return self.total(0)


def local(
    tokens, gain_one, shift_one, w_query, b_query, w_key, w_value, b_value, w_out, b_out,
    gain_two, shift_two, w_up, b_up, w_down, b_down, cotangent, plan=None,
):
    images, ranks, n_dp = plan.images, plan.ranks, plan.n_dp
    shard_rows = w_query.shape[0]
    width = tokens.shape[1]
    head_cols, hidden_cols = w_query.shape[1], w_up.shape[1]
    heads = head_cols // HD
    me_t = lax.axis_index("tensor")
    me_image, me_rank = me_t // ranks, me_t % ranks

    def shard_of(i):
        return (me_image ^ i) * ranks + me_rank

    def columns(vector, cols):
        return [lax.dynamic_slice_in_dim(vector, shard_of(i) * cols, cols) for i in range(images)]

    def uncolumns(parts, length):
        cols = parts[0].shape[0]
        blank = jnp.zeros((length,), F32)
        for i in range(images):
            blank = lax.dynamic_update_slice_in_dim(blank, parts[i], shard_of(i) * cols, 0)
        return blank

    order = Order()

    def scatter(lefts, rights, name, way="far"):
        table = plan.slots(way).reshape(-1)
        keep, send = weight_grad(order.enter(table), lefts, rights, n_dp, name)
        order.leave(send)
        begun = Scatter(plan, order, keep, send, way)
        begun.to(plan.stages - 1)
        return begun

    def low(values):
        return values.astype(LOW)

    each = range(images)
    last, near = plan.stages, max(plan.stages - 1, 0)
    far = max(plan.stages - 2, 0)
    first = max(plan.stages - 3, 0)
    gather_qkv = Gather(plan, order, low(jnp.concatenate([w_query, w_key, w_value], axis=1)))
    gather_out = Gather(plan, order, low(w_out).T)
    gather_up = Gather(plan, order, low(w_up))
    gather_down = Gather(plan, order, low(w_down).T, "near", joined=False)
    cot_rows = plan.rank_gather(cotangent)
    inputs32 = tokens.astype(F32)
    normed_one = low(layer_norm(inputs32, gain_one, shift_one))
    rows_one = plan.rank_gather(normed_one)
    token = gather_qkv.to(first)
    down_token = gather_down.to(min(1, far))
    gather_qkv.to(far)
    out_token = gather_out.to(first, token)
    token = gather_qkv.held[-1]
    gather_qkv.to(near, out_token, down_token, rows_one[-1], cot_rows[-1])
    up_token = gather_up.to(first, token)
    out_token = gather_out.to(far, token)
    token = gather_qkv.held[-1]
    gather_qkv.to(last, out_token, up_token)
    gather_up.to(far, token)
    gather_out.to(near, gather_qkv.held[-1])
    gather_up.to(near, gather_qkv.held[-1])
    gather_down.to(near - 1, gather_up.held[0])
    order.begun = [gather_up.held[0], gather_down.held[0]]

    query_bias, value_bias = columns(b_query, head_cols), columns(b_value, head_cols)
    blank = jnp.zeros((head_cols,), F32)
    qkv, mixed, lse, qkv_full = [None] * images, [None] * images, [None] * images, [None] * images
    for i in each:
        bias = order.enter(jnp.concatenate([query_bias[i], blank, value_bias[i]])[None])
        qkv[i], mixed[i], lse[i], qkv_full[i] = attend_forward(bias, rows_one, gather_qkv.weight(), i, heads)
        order.leave(lse[i])
        if i == 0:
            gather_out.to(last)
            gather_up.to(last)
            gather_down.to(near)

    out_full = [placed(gather_out.weight(), order.enter, i, "place_out") for i in each]
    attn = sum(dot(mixed[i], out_full[i], NT) for i in each)
    order.leave(attn[:8])
    gather_down.to(last)
    (attn,) = tie((order.enter(attn),), [gather_up.held[-1]])
    residual = inputs32 + plan.rank_scatter(attn) + b_out
    normed_two = low(layer_norm(residual, gain_two, shift_two))
    order.leave(normed_two[:8])
    rows_two = plan.rank_gather(normed_two)
    up_bias = columns(b_up, hidden_cols)
    act, slope, up_full = [None] * images, [None] * images, [None] * images
    for i in each:
        bias = order.enter(up_bias[i][None])
        act[i], slope[i], up_full[i] = up(bias, rows_two, gather_up.weight(), i)
        order.leave(act[i])
    scatter_down = scatter(cot_rows, act, "grad_down", "near")

    grad_out = cotangent.astype(F32)
    down_bias_grad = jnp.sum(grad_out, axis=0)
    pre_low, up_bias_parts, down_full = [None] * images, [None] * images, [None] * images
    down_weight = gather_down.weight()
    for i in each:
        table = order.enter(down_weight.table[i])
        pre_low[i], up_bias_parts[i], down_full[i] = pre_grad(table, slope[i], cot_rows, down_weight)
        order.leave(up_bias_parts[i])
    partial_two = sum(dot(pre_low[i], up_full[i], NT) for i in each)
    order.leave(partial_two[:8])
    scatter_up = scatter(rows_two, pre_low, "grad_up")
    scatter_down.to(far)
    (partial_two,) = tie((partial_two,), [scatter_down.send])
    norm_two_grad = plan.rank_scatter(partial_two)
    _, pull_two = jax.vjp(layer_norm, residual, gain_two, shift_two)
    residual_part, gain_two_grad, shift_two_grad = pull_two(norm_two_grad)
    residual_grad = grad_out + residual_part
    branch_low = low(residual_grad)
    out_bias_grad = jnp.sum(branch_low, axis=0, dtype=F32)
    branch_rows = plan.rank_gather(branch_low)
    scatter_out = scatter(branch_rows, mixed, "grad_out")

    qkv_grads = []
    for i in each:
        start = order.enter(lse[i])
        qkv_grads.append(attend_backward(start, qkv[i], mixed[i], out_full[i], branch_rows, heads))
        order.leave(qkv_grads[i])
        if i == 0:
            scatter_down.to(first)
            scatter_up.to(far)
            scatter_out.to(far)
    scatter_qkv = scatter(rows_one, qkv_grads, "grad_qkv")
    scatter_up.to(first)
    scatter_out.to(first)
    scatter_down.to(0)
    partial_one = sum(dot(order.enter(qkv_grads[i]), qkv_full[i], NT) for i in each)
    order.leave(partial_one[:8])
    down_grad = scatter_down.finish(*order.done)
    order.begun.append(down_grad)
    mlp = sum(dot(order.enter(act[i]), down_full[i], NT) for i in each)
    order.leave(mlp[:8])
    scatter_up.to(0)
    scatter_out.to(0)
    mlp = plan.rank_scatter(mlp)
    (norm_one_grad,) = tie((order.enter(plan.rank_scatter(partial_one)),), [mlp])
    _, pull_one = jax.vjp(layer_norm, inputs32, gain_one, shift_one)
    input_part, gain_one_grad, shift_one_grad = pull_one(norm_one_grad)
    grad_tokens = low(residual_grad + input_part)
    output = low(residual + mlp + b_down)
    order.leave(gain_one_grad)
    scatter_qkv.to(far)
    up_grad = scatter_up.finish()
    out_grad = scatter_out.finish().T
    down_grad = down_grad.T
    gain_one_grad = order.enter(gain_one_grad)
    qkv_sums = [jnp.sum(grads, axis=0, dtype=F32) for grads in qkv_grads]
    up_bias_grad = uncolumns([order.enter(part)[0] for part in up_bias_parts], b_up.shape[0])
    query_bias_grad = uncolumns([sums[:head_cols] for sums in qkv_sums], b_query.shape[0])
    value_bias_grad = uncolumns([sums[2 * head_cols :] for sums in qkv_sums], b_value.shape[0])

    vectors = [
        gain_one_grad, shift_one_grad, query_bias_grad, value_bias_grad, out_bias_grad,
        gain_two_grad, shift_two_grad, up_bias_grad, down_bias_grad,
    ]
    lengths = [vector.shape[0] for vector in vectors]
    together = jnp.concatenate([*vectors, jnp.zeros((-sum(lengths) % 1024,), F32)])
    for stage in range(plan.rank_stages):
        together = together + plan.rank_exchange(together, stage)
    for stage in range(plan.stages):
        together = together + plan.exchange(together, stage)
        if stage in (first - 1, first):
            order.leave(together)
            if stage == first - 1:
                scatter_qkv.to(first, up_grad, out_grad)
            else:
                scatter_qkv.to(0)
            together = order.enter(together)
    qkv_grad = scatter_qkv.finish()
    query_grad, key_grad, value_grad = (qkv_grad[:, n * head_cols : (n + 1) * head_cols] for n in range(3))
    small, begin = [], 0
    for length in lengths:
        small.append(together[begin : begin + length])
        begin += length
    return (
        output, grad_tokens, small[0], small[1], query_grad, small[2], key_grad, value_grad, small[3],
        out_grad, small[4], small[5], small[6], up_grad, small[7], down_grad, small[8],
    )


def solution(mesh):
    split = P(("dp", "tensor"), None)
    whole, wide, tall = P(), P("dp", "tensor"), P("tensor", "dp")
    n_dp, n_t = mesh.shape["dp"], mesh.shape["tensor"]

    def layer(*args):
        rows = args[0].shape[0] // (n_dp * n_t)
        plan = Plan(n_dp, n_t, LEN // rows)
        return jax.shard_map(
            functools.partial(local, plan=plan),
            mesh=mesh,
            in_specs=(
                split, whole, whole, wide, whole, wide, wide, whole, tall, whole,
                whole, whole, wide, whole, tall, whole, split,
            ),
            out_specs=(
                split, split, whole, whole, wide, whole, wide, wide, whole,
                tall, whole, whole, whole, wide, whole, tall, whole,
            ),
            check_vma=False,
        )(*args)

    return layer
```
